32 devices in a mesh: tx: 8 (over y, x, core), ty: 4 (over z).
Axes of the slice: x: 2, y: 2, z: 4, core: 2. Of those that a mesh axis runs over, the one named last changes fastest.
Arguments:
- volume: bfloat16 [256, 128, 16, 64], P('tx', 'ty'), may hold values from -6 to 6
- first_weight: bfloat16 [2, 2, 2, 64, 128], replicated, may hold values from -0.375 to 0.375
- first_bias: float32 [128], replicated, may hold values from -1.5 to 1.5
- second_weight: bfloat16 [2, 2, 2, 128, 256], replicated, may hold values from -0.25 to 0.25
- second_bias: float32 [256], replicated, may hold values from -1.5 to 1.5
- inner_weight: bfloat16 [3, 3, 3, 256, 256], replicated, may hold values from -0.109375 to 0.109375
- inner_bias: float32 [256], replicated, may hold values from -1.5 to 1.5
- outer_weight: bfloat16 [3, 3, 3, 256, 256], replicated, may hold values from -0.109375 to 0.109375
- outer_bias: float32 [256], replicated, may hold values from -1.5 to 1.5
Outputs:
- encoded: bfloat16 [64, 32, 4, 256], P('tx', 'ty')
The draws below stay inside these ranges and needn't reach their ends.
All inputs are finite; a program needn't handle non-finite values.
Results may differ from the reference program's by a relative error of at most 0.0058.
Values may be sent and summed in bfloat16 or wider, within the bound.
A program may use at most 64 MiB of HBM per device.

```python
import jax
import jax.numpy as jnp
from jax import lax

CIN = 64
C1 = 128
C2 = 256
DILATION_RATE = 2
FZ = 16
NX = 256
NY = 128
KX = 64
KY = 32
KZ = 4


def level_of(own_key, extent, cuts, low, top_value):
    def one(dim, shards_of):
        draws = jax.random.uniform(jax.random.fold_in(jax.random.fold_in(own_key, 6), dim), (shards_of,), jnp.float32, low / len(cuts), top_value / len(cuts))
        return jnp.repeat(jnp.exp(draws), extent[dim] // shards_of).reshape((-1,) + (1,) * (len(extent) - dim - 1))

    loudness = one(*cuts[0])
    for cut in cuts[1:]:
        loudness = loudness * one(*cut)
    return loudness


def scatter_about(key, shape, scale, bound, cuts=(), dtype=jnp.bfloat16):
    values = jax.random.normal(key, shape, jnp.float32) * scale
    if len(cuts) > 0:
        values = level_of(key, shape, cuts, -0.22, 0.18) * values
    return jnp.clip(values, min=-bound, max=bound).astype(dtype)


def setup_inputs(seed: int = 0) -> dict:
    seeds = jax.random.split(jax.random.key(seed), 10)
    return {
        "volume": scatter_about(seeds[0], (NX, NY, FZ, CIN), 1.0, 6.0, ((0, 8), (1, 4))),
        "first_weight": scatter_about(seeds[1], (2, 2, 2, CIN, C1), (4 * CIN) ** -0.5, 0.375),
        "first_bias": scatter_about(seeds[2], (C1,), 0.3, 1.5, (), jnp.float32),
        "second_weight": scatter_about(seeds[3], (2, 2, 2, C1, C2), (4 * C1) ** -0.5, 0.25),
        "second_bias": scatter_about(seeds[4], (C2,), 0.3, 1.5, (), jnp.float32),
        "inner_weight": scatter_about(seeds[5], (3, 3, 3, C2, C2), (27 * C2 // 2) ** -0.5, 0.109375),
        "inner_bias": scatter_about(seeds[6], (C2,), 0.3, 1.5, (), jnp.float32),
        "outer_weight": scatter_about(seeds[7], (3, 3, 3, C2, C2), (27 * C2 // 2) ** -0.5, 0.109375),
        "outer_bias": scatter_about(seeds[8], (C2,), 0.3, 1.5, (), jnp.float32),
    }


def leaky(values):
    return jnp.where(values > 0, values, 0.01 * values)


def strided(feature_field, weight, bias):
    size_x, size_y, size_z, chans = feature_field.shape
    blocks = feature_field.reshape(size_x // 2, 2, size_y // 2, 2, size_z // 2, 2, chans)
    blocks = blocks.transpose(0, 2, 4, 1, 3, 5, 6).reshape(-1, 8 * chans)
    total = jnp.dot(blocks, weight.reshape(8 * chans, -1), preferred_element_type=jnp.float32)
    return leaky(total + bias).astype(jnp.bfloat16).reshape(size_x // 2, size_y // 2, size_z // 2, -1)


def dilated_sum(padded_volume, weight):
    output_x = padded_volume.shape[0] - 2 * DILATION_RATE
    output_y = padded_volume.shape[1] - 2 * DILATION_RATE
    output_z = padded_volume.shape[2] - 2 * DILATION_RATE
    chans = padded_volume.shape[3]
    total = jnp.zeros((output_x * output_y * output_z, weight.shape[4]), jnp.float32)
    for shift_along_x in range(3):
        for shift_along_y in range(3):
            for shift_along_z in range(3):
                volume_portion = padded_volume[shift_along_x * DILATION_RATE:shift_along_x * DILATION_RATE + output_x, shift_along_y * DILATION_RATE:shift_along_y * DILATION_RATE + output_y, shift_along_z * DILATION_RATE:shift_along_z * DILATION_RATE + output_z, :]
                total = total + jnp.dot(volume_portion.reshape(-1, chans), weight[shift_along_x, shift_along_y, shift_along_z], preferred_element_type=jnp.float32)
    return total.reshape(output_x, output_y, output_z, -1)


def pad_all(feature_field):
    return jnp.pad(feature_field, ((DILATION_RATE, DILATION_RATE), (DILATION_RATE, DILATION_RATE), (DILATION_RATE, DILATION_RATE), (0, 0)))


def reference(volume, first_weight, first_bias, second_weight, second_bias, inner_weight, inner_bias, outer_weight, outer_bias):
    def section(slab):
        return strided(strided(slab, first_weight, first_bias), second_weight, second_bias)

    coarse_volume = lax.map(section, volume.reshape(NX // 32, 32, NY, FZ, CIN)).reshape(KX, KY, KZ, C2)
    hidden_activation = leaky(dilated_sum(pad_all(coarse_volume), inner_weight) + inner_bias).astype(jnp.bfloat16)
    result = leaky(coarse_volume.astype(jnp.float32) + dilated_sum(pad_all(hidden_activation), outer_weight) + outer_bias)
    return result.astype(jnp.bfloat16)
```

```python
import jax
import jax.numpy as jnp
from jax import lax
from jax.experimental import pallas as pl
from jax.experimental.pallas import tpu as pltpu
from jax.sharding import PartitionSpec as P

MESSAGES = (
    (-1, 0, 0), (1, 0, 1),
    (-1, -1, 0), (-1, 1, 0), (0, -1, 0), (0, 1, 0),
    (1, -1, 1), (1, 1, 1), (0, -1, 1), (0, 1, 1),
)
PARTNER = (1, 0, 7, 6, 5, 4, 3, 2, 9, 8)
FIRST = (2, 3, 4, 5, 0)
SECOND = (6, 7, 8, 9, 1)
NEIGHBOURS = (0, 1, 2, 3, 4, 5, 6, 7)
BF = jnp.bfloat16
F32 = jnp.float32


def leaky(values):
    return jnp.where(values > 0, values, 0.01 * values)


def kernel(
    volume, w1, b1, w2, b2, wi, bi, wo, bo,
    out,
    vbuf, w1b, w2b, wib, wob, b1b, b2b, bib, bob,
    sums, blocks, halo, inner, edge_out, edge_in, corner_out, corner_in,
    load_sem, send_sem, recv_sem,
):
    ix, iy = lax.axis_index("tx"), lax.axis_index("ty")
    nx, ny = lax.axis_size("tx"), lax.axis_size("ty")
    groups_x, groups_y = halo.shape[1] - 4, halo.shape[2] - 4
    half = groups_x * groups_y * 8

    def exists(d):
        dx, dy, _ = MESSAGES[d]
        test = None
        for delta, i, n in ((dx, ix, nx), (dy, iy, ny)):
            if delta:
                one = i >= 1 if delta < 0 else i <= n - 2
                test = one if test is None else jnp.logical_and(test, one)
        return test

    def device(d):
        return {"tx": ix + MESSAGES[d][0], "ty": iy + MESSAGES[d][1]}

    loads = []

    def load(src, dst):
        copy = pltpu.make_async_copy(src, dst, load_sem.at[len(loads)])
        copy.start()
        loads.append(copy)
        return copy

    load_w1, load_b1 = load(w1, w1b), load(b1, b1b)
    load_v = [load(volume.at[pl.ds(8 * i, 8)], vbuf.at[i]) for i in range(groups_x)]
    load_w2, load_b2 = load(w2, w2b), load(b2, b2b)
    load_bi, load_bo = load(bi, bib), load(bo, bob)
    load_wi = {a: load(wi.at[a], wib.at[a]) for a in (1, 0, 2)}
    load_wo = {a: load(wo.at[a], wob.at[a]) for a in (1, 0, 2)}

    barrier = pltpu.get_barrier_semaphore()
    count = 0
    for d in NEIGHBOURS:
        count = count + exists(d).astype(jnp.int32)

        @pl.when(exists(d))
        def _():
            pl.semaphore_signal(
                barrier, inc=1, device_id=device(d), device_id_type=pl.DeviceIdType.MESH
            )

    halo[...] = jnp.zeros_like(halo)

    load_w1.wait()
    load_b1.wait()
    w1cat = jnp.concatenate(
        [
            jnp.concatenate([w1b[p, q, 0], w1b[p, q, 1]], axis=1)
            for p in range(2)
            for q in range(2)
        ],
        axis=0,
    )
    rows_y = 2 * groups_y
    bias1 = b1b[...]
    def first(i):
        load_v[i].wait()
        for xp in range(2):
            slabs = [
                vbuf[i, 4 * xp + j].reshape(rows_y, 4, 16, 64) for j in range(4)
            ]
            for pc in range(2):
                for qc in range(2):
                    lhs = jnp.concatenate(
                        [
                            slabs[2 * pc + p][:, 2 * qc + q].reshape(rows_y * 16, 64)
                            for p in range(2)
                            for q in range(2)
                        ],
                        axis=1,
                    )
                    slot = (i * 2 + xp) * 4 + pc * 2 + qc
                    both = jnp.dot(lhs, w1cat, preferred_element_type=F32)
                    sums[slot, 0] = both[:, 0:128]
                    sums[slot, 1] = both[:, 128:256]
            for pc in range(2):
                for qc in range(2):
                    slot = (i * 2 + xp) * 4 + pc * 2 + qc
                    for rc in range(2):
                        even = sums[slot, 0, pl.ds(2 * rc, 4 * rows_y, stride=4)]
                        odd = sums[slot, 1, pl.ds(2 * rc + 1, 4 * rows_y, stride=4)]
                        finer = leaky(even + odd + bias1).astype(BF)
                        k = (pc * 2 + qc) * 2 + rc
                        row = (i * 2 + xp) * 4 * rows_y
                        blocks[row : row + 4 * rows_y, k * 128 : k * 128 + 128] = finer

    def copy_of(d, incoming):
        slot = d if incoming else PARTNER[d]
        if d < 2:
            src, dst = edge_out.at[d], edge_in.at[slot]
        else:
            src, dst = corner_out.at[d - 2], corner_in.at[slot - 2]
        return pltpu.make_async_remote_copy(
            src_ref=src,
            dst_ref=dst,
            send_sem=send_sem.at[d],
            recv_sem=recv_sem.at[slot],
            device_id=device(d),
            device_id_type=pl.DeviceIdType.MESH,
        )

    def landed(d):
        dx, dy, h = MESSAGES[d]
        if dx:
            px = slice(0, 2) if dx < 0 else slice(groups_x + 2, groups_x + 4)
        else:
            px = slice(2 + 2 * h, 4 + 2 * h)
        if dy:
            return px, slice(0, 2) if dy < 0 else slice(groups_y + 2, groups_y + 4)
        return px, slice(2, 2 + groups_y)

    def second(h):
        rows = half
        total = jnp.dot(
            blocks[h * rows : h * rows + rows],
            w2b[...].reshape(8 * 128, 256),
            preferred_element_type=F32,
        )
        coarse = leaky(total + b2b[...]).astype(BF).astype(F32)
        coarse = coarse.reshape(groups_x // 2, 2, groups_y * 8, 256)
        rows = half // 2
        even_x = coarse[:, 0].reshape(rows, 256)
        odd_x = coarse[:, 1].reshape(rows, 256)
        keep = (lax.broadcasted_iota(jnp.int32, (rows, 256), 0) // 2) % 2 == 0
        parts = [
            part.reshape(groups_x // 2, groups_y, 8, 256)
            for part in (
                jnp.where(keep, even_x, pltpu.roll(odd_x, 2, 0)),
                jnp.where(keep, pltpu.roll(even_x, rows - 2, 0), odd_x),
            )
        ]
        for d in SECOND if h else FIRST:
            dy = MESSAGES[d][1]
            sy = slice(0, 2) if dy < 0 else slice(groups_y - 2, groups_y) if dy else slice(0, groups_y)
            block = jnp.concatenate([p[:, sy].reshape(-1, 256) for p in parts], axis=0).astype(BF)
            if d < 2:
                edge_out[d] = block
            else:
                corner_out[d - 2] = block

            @pl.when(exists(d))
            def _():
                copy_of(d, False).start()

        for z in range(2):
            halo[z, 2 + 2 * h : 4 + 2 * h, 2 : 2 + groups_y] = parts[z]

    per_half = groups_x // 2
    for i in range(per_half):
        first(i)
    load_w2.wait()
    load_b2.wait()
    pl.semaphore_wait(barrier, count)
    second(0)
    for i in range(per_half, groups_x):
        first(i)
    second(1)

    own = jnp.concatenate(
        [
            halo[z, 2 : 2 + groups_x, 2 : 2 + groups_y].reshape(half, 256).astype(BF)
            for z in range(2)
        ],
        axis=1,
    )
    keep = (lax.broadcasted_iota(jnp.int32, (half, 256), 0) // 2) % 2 == 0
    load_bi.wait()
    load_bo.wait()
    inner[...] = jnp.broadcast_to(bib[...].reshape(1, 1, 1, 1, 256), inner.shape)

    def both(lhs, weight, a, b):
        lower = weight[a, b, 1:3].reshape(512, 256)
        upper = weight[a, b, 0:2].reshape(512, 256)
        return (
            jnp.dot(lhs, lower, preferred_element_type=F32),
            jnp.dot(lhs, upper, preferred_element_type=F32),
        )

    for a in (1, 0, 2):
        load_wi[a].wait()
        for b in (1, 0, 2):
            for z, term in enumerate(both(own, wib, a, b)):
                inner[z, 2 - a : 2 - a + groups_x, 2 - b : 2 - b + groups_y] += term.reshape(
                    groups_x, groups_y, 8, 256
                )

    for d in FIRST + SECOND:
        px, py = landed(d)

        @pl.when(exists(d))
        def _():
            copy_of(d, True).wait_recv()
            block = (edge_in[d] if d < 2 else corner_in[d - 2]).astype(F32)
            rows = block.shape[0] // 2
            for z in range(2):
                shape = (px.stop - px.start, py.stop - py.start, 8, 256)
                halo[z, px, py] = block[z * rows : z * rows + rows].reshape(shape)

    def outside(shift, groups):
        return [i for i in range(shift, shift + groups + 2) if not 2 <= i < 2 + groups]

    for a in (1, 0, 2):
        for b in (1, 0, 2):
            pieces = [
                (slice(i, i + 1), slice(b, b + groups_y + 2)) for i in outside(a, groups_x)
            ] + [
                (slice(2, 2 + groups_x), slice(i, i + 1)) for i in outside(b, groups_y)
            ]
            lhs = jnp.concatenate(
                [
                    jnp.concatenate(
                        [halo[z, sx, sy].reshape(-1, 256) for sx, sy in pieces], axis=0
                    ).astype(BF)
                    for z in range(2)
                ],
                axis=1,
            )
            for z, term in enumerate(both(lhs, wib, a, b)):
                row = 0
                for sx, sy in pieces:
                    shape = (sx.stop - sx.start, sy.stop - sy.start, 8, 256)
                    rows = shape[0] * shape[1] * 8
                    inner[
                        z, sx.start - a : sx.stop - a, sy.start - b : sy.stop - b
                    ] += term[row : row + rows].reshape(shape)
                    row += rows

    inner[...] = leaky(inner[...]).astype(BF).astype(F32)

    @pl.when(ix == 0)
    def _():
        inner[:, 0] = jnp.zeros_like(inner[:, 0])

    @pl.when(ix == nx - 1)
    def _():
        inner[:, groups_x + 1] = jnp.zeros_like(inner[:, 0])

    @pl.when(iy == 0)
    def _():
        inner[:, :, 0] = jnp.zeros_like(inner[:, :, 0])

    @pl.when(iy == ny - 1)
    def _():
        inner[:, :, groups_y + 1] = jnp.zeros_like(inner[:, :, 0])

    totals = [
        halo[z, 2 : 2 + groups_x, 2 : 2 + groups_y].reshape(half, 256) + bob[...]
        for z in range(2)
    ]
    for a in (1, 0, 2):
        load_wo[a].wait()
        for b in (1, 0, 2):
            lhs = jnp.concatenate(
                [
                    inner[z, a : a + groups_x, b : b + groups_y].reshape(half, 256).astype(BF)
                    for z in range(2)
                ],
                axis=1,
            )
            totals = [t + term for t, term in zip(totals, both(lhs, wob, a, b))]
    lower, upper = leaky(totals[0]), leaky(totals[1])
    even_x = jnp.where(keep, lower, pltpu.roll(upper, 2, 0)).astype(BF)
    odd_x = jnp.where(keep, pltpu.roll(lower, half - 2, 0), upper).astype(BF)
    rows = groups_y * 8
    for i in range(groups_x):
        for p, part in enumerate((even_x, odd_x)):
            out[2 * i + p] = part[i * rows : (i + 1) * rows].reshape(2 * groups_y, 4, 256)

    for d in range(10):

        @pl.when(exists(d))
        def _():
            copy_of(d, False).wait_send()


def local(
    volume,
    first_weight,
    first_bias,
    second_weight,
    second_bias,
    inner_weight,
    inner_bias,
    outer_weight,
    outer_bias,
):
    size_x, size_y, size_z, chans = volume.shape
    gx, gy = size_x // 8, size_y // 8
    cells = gx * gy * 16
    any_spec = pl.BlockSpec(memory_space=pl.ANY)
    vmem = pltpu.VMEM
    result = pl.pallas_call(
        kernel,
        out_shape=pltpu.VMEM((size_x // 4, size_y // 4, size_z // 4, 256), BF),
        in_specs=[any_spec] * 9,
        out_specs=pl.BlockSpec(memory_space=pltpu.VMEM),
        scratch_shapes=[
            vmem((gx, 8, size_y, size_z, chans), BF),
            vmem(first_weight.shape, BF),
            vmem(second_weight.shape, BF),
            vmem(inner_weight.shape, BF),
            vmem(outer_weight.shape, BF),
            vmem((1, 128), F32),
            vmem((1, 256), F32),
            vmem((1, 256), F32),
            vmem((1, 256), F32),
            vmem((gx * 8, 2, gy * 32, 128), F32),
            vmem((cells, 1024), BF),
            vmem((2, gx + 4, gy + 4, 8, 256), F32),
            vmem((2, gx + 2, gy + 2, 8, 256), F32),
            vmem((2, gy * 32, 256), BF),
            vmem((2, gy * 32, 256), BF),
            vmem((8, 64, 256), BF),
            vmem((8, 64, 256), BF),
            pltpu.SemaphoreType.DMA((gx + 12,)),
            pltpu.SemaphoreType.DMA((10,)),
            pltpu.SemaphoreType.DMA((10,)),
        ],
        compiler_params=pltpu.CompilerParams(
            collective_id=0, has_side_effects=True, vmem_limit_bytes=56 * 2**20
        ),
        cost_estimate=pl.CostEstimate(
            flops=2_000_000_000, bytes_accessed=12_000_000, transcendentals=0
        ),
    )(
        volume,
        first_weight,
        first_bias.reshape(1, -1),
        second_weight,
        second_bias.reshape(1, -1),
        inner_weight,
        inner_bias.reshape(1, -1),
        outer_weight,
        outer_bias.reshape(1, -1),
    )
    return result


def solution(mesh):
    in_specs = (P("tx", "ty", None, None), P(), P(), P(), P(), P(), P(), P(), P())
    out_specs = P("tx", "ty", None, None)
    return jax.shard_map(local, mesh=mesh, in_specs=in_specs, out_specs=out_specs, check_vma=False)
```

```python
import jax
import jax.numpy as jnp
from jax import lax
from jax.experimental import pallas as pl
from jax.experimental.pallas import tpu as pltpu
from jax.sharding import PartitionSpec as P

MESSAGES = (
    (-1, 0, 0), (1, 0, 1),
    (-1, -1, 0), (-1, 1, 0), (0, -1, 0), (0, 1, 0),
    (1, -1, 1), (1, 1, 1), (0, -1, 1), (0, 1, 1),
)
PARTNER = (1, 0, 7, 6, 5, 4, 3, 2, 9, 8)
FIRST = (2, 3, 4, 5, 0)
SECOND = (8, 9, 6, 7, 1)
NEIGHBOURS = (0, 1, 2, 3, 4, 5, 6, 7)
BF = jnp.bfloat16
F32 = jnp.float32


def leaky(values):
    return jnp.where(values > 0, values, 0.01 * values)


def kernel(
    volume, w1, b1, w2, b2, wi, bi, wo, bo,
    out,
    vbuf, w1b, w2b, wib, wob, b1b, b2b, bib, bob,
    lhs, sums, blocks, halo, inner, edge_out, edge_in, corner_out, corner_in,
    load_sem, send_sem, recv_sem,
):
    ix, iy = lax.axis_index("tx"), lax.axis_index("ty")
    nx, ny = lax.axis_size("tx"), lax.axis_size("ty")
    groups_x, groups_y = halo.shape[1] - 4, halo.shape[2] - 4
    half = groups_x * groups_y * 8

    def exists(d):
        dx, dy, _ = MESSAGES[d]
        test = None
        for delta, i, n in ((dx, ix, nx), (dy, iy, ny)):
            if delta:
                one = i >= 1 if delta < 0 else i <= n - 2
                test = one if test is None else jnp.logical_and(test, one)
        return test

    def device(d):
        return {"tx": ix + MESSAGES[d][0], "ty": iy + MESSAGES[d][1]}

    barrier = pltpu.get_barrier_semaphore()
    count = 0
    for d in NEIGHBOURS:
        count = count + exists(d).astype(jnp.int32)

        @pl.when(exists(d))
        def _():
            pl.semaphore_signal(
                barrier, inc=1, device_id=device(d), device_id_type=pl.DeviceIdType.MESH
            )

    loads = []

    def load(src, dst):
        copy = pltpu.make_async_copy(src, dst, load_sem.at[len(loads)])
        copy.start()
        loads.append(copy)
        return copy

    load_w1, load_b1 = load(w1, w1b), load(b1, b1b)
    units = vbuf.shape[0]
    load_v = [load(volume.at[pl.ds(4 * u, 4)], vbuf.at[u]) for u in range(units // 2)]
    load_w2, load_b2 = load(w2, w2b), load(b2, b2b)
    load_v += [load(volume.at[pl.ds(4 * u, 4)], vbuf.at[u]) for u in range(units // 2, units)]
    load_bi, load_bo = load(bi, bib), load(bo, bob)
    load_wi = {a: load(wi.at[a], wib.at[a]) for a in (1, 0, 2)}
    load_wo = {a: load(wo.at[a], wob.at[a]) for a in (1, 0, 2)}

    halo[...] = jnp.zeros_like(halo)

    load_w1.wait()
    load_b1.wait()
    w1cat = jnp.concatenate(
        [
            jnp.concatenate([w1b[p, q, 0], w1b[p, q, 1]], axis=1)
            for p in range(2)
            for q in range(2)
        ],
        axis=0,
    )
    rows_y = 2 * groups_y
    bias1 = b1b[...]

    def gather(u):
        slabs = [vbuf[u, j].reshape(rows_y, 4, 16, 64) for j in range(4)]
        for pc in range(2):
            for qc in range(2):
                lhs[u % 2, pc * 2 + qc] = jnp.concatenate(
                    [
                        slabs[2 * pc + p][:, 2 * qc + q].reshape(rows_y * 16, 64)
                        for p in range(2)
                        for q in range(2)
                    ],
                    axis=1,
                )

    def multiply(u):
        for k in range(4):
            both = jnp.dot(lhs[u % 2, k], w1cat, preferred_element_type=F32)
            sums[u * 4 + k, 0] = both[:, 0:128]
            sums[u * 4 + k, 1] = both[:, 128:256]

    def fold(u):
        row = u * 4 * rows_y
        for k in range(8):
            slot, rc = u * 4 + k // 2, k % 2
            even = sums[slot, 0, pl.ds(2 * rc, 4 * rows_y, stride=4)]
            odd = sums[slot, 1, pl.ds(2 * rc + 1, 4 * rows_y, stride=4)]
            finer = leaky(even + odd + bias1).astype(BF)
            blocks[row : row + 4 * rows_y, k * 128 : k * 128 + 128] = finer

    def copy_of(d, incoming):
        slot = d if incoming else PARTNER[d]
        if d < 2:
            src, dst = edge_out.at[d], edge_in.at[slot]
        else:
            src, dst = corner_out.at[d - 2], corner_in.at[slot - 2]
        return pltpu.make_async_remote_copy(
            src_ref=src,
            dst_ref=dst,
            send_sem=send_sem.at[d],
            recv_sem=recv_sem.at[slot],
            device_id=device(d),
            device_id_type=pl.DeviceIdType.MESH,
        )

    def landed(d):
        dx, dy, h = MESSAGES[d]
        if dx:
            px = slice(0, 2) if dx < 0 else slice(groups_x + 2, groups_x + 4)
        else:
            px = slice(2 + 2 * h, 4 + 2 * h)
        if dy:
            return px, slice(0, 2) if dy < 0 else slice(groups_y + 2, groups_y + 4)
        return px, slice(2, 2 + groups_y)

    def second(h):
        rows = half
        total = jnp.dot(
            blocks[h * rows : h * rows + rows],
            w2b[...].reshape(8 * 128, 256),
            preferred_element_type=F32,
        )
        coarse = leaky(total + b2b[...]).astype(BF).astype(F32)
        coarse = coarse.reshape(groups_x // 2, 2, groups_y * 8, 256)
        rows = half // 2
        even_x = coarse[:, 0].reshape(rows, 256)
        odd_x = coarse[:, 1].reshape(rows, 256)
        keep = (lax.broadcasted_iota(jnp.int32, (rows, 256), 0) // 2) % 2 == 0
        parts = [
            part.reshape(groups_x // 2, groups_y, 8, 256)
            for part in (
                jnp.where(keep, even_x, pltpu.roll(odd_x, 2, 0)),
                jnp.where(keep, pltpu.roll(even_x, rows - 2, 0), odd_x),
            )
        ]
        for d in SECOND if h else FIRST:
            dy = MESSAGES[d][1]
            sy = slice(0, 2) if dy < 0 else slice(groups_y - 2, groups_y) if dy else slice(0, groups_y)
            block = jnp.concatenate([p[:, sy].reshape(-1, 256) for p in parts], axis=0).astype(BF)
            if d < 2:
                edge_out[d] = block
            else:
                corner_out[d - 2] = block

            @pl.when(exists(d))
            def _():
                copy_of(d, False).start()

        for z in range(2):
            halo[z, 2 + 2 * h : 4 + 2 * h, 2 : 2 + groups_y] = parts[z]

    for t in range(units + 2):
        if t < units:
            load_v[t].wait()
            gather(t)
        if 1 <= t <= units:
            multiply(t - 1)
        if 2 <= t:
            fold(t - 2)
        if t == units // 2 + 1:
            load_w2.wait()
            load_b2.wait()
            pl.semaphore_wait(barrier, count)
            second(0)
        if t == units + 1:
            second(1)

    own = jnp.concatenate(
        [
            halo[z, 2 : 2 + groups_x, 2 : 2 + groups_y].reshape(half, 256).astype(BF)
            for z in range(2)
        ],
        axis=1,
    )
    keep = (lax.broadcasted_iota(jnp.int32, (half, 256), 0) // 2) % 2 == 0
    load_bi.wait()
    load_bo.wait()
    inner[...] = jnp.broadcast_to(bib[...].reshape(1, 1, 1, 1, 256), inner.shape)

    def both(lhs, weight, a, b):
        lower = weight[a, b, 1:3].reshape(512, 256)
        upper = weight[a, b, 0:2].reshape(512, 256)
        return (
            jnp.dot(lhs, lower, preferred_element_type=F32),
            jnp.dot(lhs, upper, preferred_element_type=F32),
        )

    for a in (1, 0, 2):
        load_wi[a].wait()
        for b in (1, 0, 2):
            for z, term in enumerate(both(own, wib, a, b)):
                inner[z, 2 - a : 2 - a + groups_x, 2 - b : 2 - b + groups_y] += term.reshape(
                    groups_x, groups_y, 8, 256
                )

    def receive(d, test=None):
        px, py = landed(d)
        there = exists(d)
        if test is not None:
            there = jnp.logical_and(there, test)

        @pl.when(there)
        def _():
            copy_of(d, True).wait_recv()
            block = (edge_in[d] if d < 2 else corner_in[d - 2]).astype(F32)
            rows = block.shape[0] // 2
            for z in range(2):
                shape = (px.stop - px.start, py.stop - py.start, 8, 256)
                halo[z, px, py] = block[z * rows : z * rows + rows].reshape(shape)

    core = lax.rem(ix, 2)

    def side(flip):
        def pick(even, odd):
            return even + flip * (odd - even)

        return (
            pick(groups_x + 2, 1),
            pick(groups_x + 3, 0),
            pick(groups_x + 1, 0),
            pick(groups_x, 1),
            pick(2, 0),
        )

    near_in, far_in, ring_in, edge_in_x, tap_in = side(core)
    near_out, far_out, ring_out, edge_out_x, tap_out = side(1 - core)

    def add(a, b, pieces):
        lhs_halo = jnp.concatenate(
            [
                jnp.concatenate(
                    [halo[z, pl.ds(g, n), sy].reshape(-1, 256) for g, n, sy, _ in pieces],
                    axis=0,
                ).astype(BF)
                for z in range(2)
            ],
            axis=1,
        )
        for z, term in enumerate(both(lhs_halo, wib, a, b)):
            row = 0
            for _, n, sy, i in pieces:
                size = sy.stop - sy.start
                inner[z, pl.ds(i, n), sy.start - b : sy.stop - b] += term[
                    row : row + n * size * 8
                ].reshape(n, size, 8, 256)
                row += n * size * 8

    def present(i, edge):
        return jnp.where(i == edge, 0.0, 1.0).astype(F32)

    scale_x = {0: present(ix, 0), groups_x + 1: present(ix, nx - 1)}
    scale_y = {0: present(iy, 0), groups_y + 1: present(iy, ny - 1)}

    def activate(rows):
        for i in rows:
            for z in range(2):
                row = leaky(inner[z, i]).astype(BF).astype(F32)
                if i in scale_x:
                    row = row * scale_x[i]
                inner[z, i] = row
                for j, scale in scale_y.items():
                    inner[z, i, j] = row[j] * scale

    own_y = slice(2, 2 + groups_y)

    def surround(cols, near, far, ring, edge, tap, other):
        for b in range(3):
            inside = [j for j in cols if b <= j < b + groups_y + 2]
            for a in (1, tap, other):
                pieces = []
                if inside:
                    strip = slice(inside[0], inside[-1] + 1)
                    pieces.append((a, groups_x + 2, strip, 0))
                if a is tap:
                    pieces += [(near, 1, own_y, edge), (far, 1, own_y, ring)]
                elif a is not other:
                    pieces.append((near, 1, own_y, ring))
                if pieces:
                    add(a, b, pieces)

    for a in (1, 0, 2):
        load_wo[a].wait()
    for d in (2, 4, 6, 8):
        receive(d)
    receive(1, core == 0)
    receive(0, core == 1)
    surround((0, 1), near_in, far_in, ring_in, edge_in_x, tap_in, tap_out)
    for d in range(10):

        @pl.when(exists(d))
        def _():
            copy_of(d, False).wait_send()

    for d in (3, 5, 7, 9):
        receive(d)
    receive(0, core == 0)
    receive(1, core == 1)
    surround(
        (groups_y + 2, groups_y + 3),
        near_out, far_out, ring_out, edge_out_x, tap_out, tap_in,
    )
    activate(range(groups_x + 2))
    totals = [
        halo[z, 2 : 2 + groups_x, own_y].reshape(half, 256) + bob[...] for z in range(2)
    ]
    for a in range(3):
        for b in range(3):
            lhs_in = jnp.concatenate(
                [
                    inner[z, a : a + groups_x, b : b + groups_y].reshape(half, 256).astype(BF)
                    for z in range(2)
                ],
                axis=1,
            )
            totals = [t + term for t, term in zip(totals, both(lhs_in, wob, a, b))]
    lower, upper = leaky(totals[0]), leaky(totals[1])
    even_x = jnp.where(keep, lower, pltpu.roll(upper, 2, 0)).astype(BF)
    odd_x = jnp.where(keep, pltpu.roll(lower, half - 2, 0), upper).astype(BF)
    rows = groups_y * 8
    for i in range(groups_x):
        for p, part in enumerate((even_x, odd_x)):
            out[2 * i + p] = part[i * rows : (i + 1) * rows].reshape(2 * groups_y, 4, 256)


def local(
    volume,
    first_weight,
    first_bias,
    second_weight,
    second_bias,
    inner_weight,
    inner_bias,
    outer_weight,
    outer_bias,
):
    size_x, size_y, size_z, chans = volume.shape
    gx, gy = size_x // 8, size_y // 8
    cells = gx * gy * 16
    any_spec = pl.BlockSpec(memory_space=pl.ANY)
    vmem = pltpu.VMEM
    result = pl.pallas_call(
        kernel,
        out_shape=pltpu.VMEM((size_x // 4, size_y // 4, size_z // 4, 256), BF),
        in_specs=[any_spec] * 9,
        out_specs=pl.BlockSpec(memory_space=pltpu.VMEM),
        scratch_shapes=[
            vmem((gx * 2, 4, size_y, size_z, chans), BF),
            vmem(first_weight.shape, BF),
            vmem(second_weight.shape, BF),
            vmem(inner_weight.shape, BF),
            vmem(outer_weight.shape, BF),
            vmem((1, 128), F32),
            vmem((1, 256), F32),
            vmem((1, 256), F32),
            vmem((1, 256), F32),
            vmem((2, 4, gy * 32, 256), BF),
            vmem((gx * 8, 2, gy * 32, 128), F32),
            vmem((cells, 1024), BF),
            vmem((2, gx + 4, gy + 4, 8, 256), F32),
            vmem((2, gx + 2, gy + 2, 8, 256), F32),
            vmem((2, gy * 32, 256), BF),
            vmem((2, gy * 32, 256), BF),
            vmem((8, 64, 256), BF),
            vmem((8, 64, 256), BF),
            pltpu.SemaphoreType.DMA((gx * 2 + 12,)),
            pltpu.SemaphoreType.DMA((10,)),
            pltpu.SemaphoreType.DMA((10,)),
        ],
        compiler_params=pltpu.CompilerParams(
            collective_id=0, has_side_effects=True, vmem_limit_bytes=56 * 2**20
        ),
        cost_estimate=pl.CostEstimate(
            flops=2_000_000_000, bytes_accessed=12_000_000, transcendentals=0
        ),
    )(
        volume,
        first_weight,
        first_bias.reshape(1, -1),
        second_weight,
        second_bias.reshape(1, -1),
        inner_weight,
        inner_bias.reshape(1, -1),
        outer_weight,
        outer_bias.reshape(1, -1),
    )
    return result


def solution(mesh):
    in_specs = (P("tx", "ty", None, None), P(), P(), P(), P(), P(), P(), P(), P())
    out_specs = P("tx", "ty", None, None)
    return jax.shard_map(local, mesh=mesh, in_specs=in_specs, out_specs=out_specs, check_vma=False)
```

```python
import jax
import jax.numpy as jnp
from jax import lax
from jax.experimental import pallas as pl
from jax.experimental.pallas import tpu as pltpu
from jax.sharding import PartitionSpec as P

MESSAGES = (
    (-1, 0, 0), (1, 0, 1),
    (-1, -1, 0), (-1, 1, 0), (0, -1, 0), (0, 1, 0),
    (1, -1, 1), (1, 1, 1), (0, -1, 1), (0, 1, 1),
)
PARTNER = (1, 0, 7, 6, 5, 4, 3, 2, 9, 8)
FIRST = (2, 3, 4, 5, 0)
SECOND = (8, 9, 6, 7, 1)
NEIGHBOURS = (0, 1, 2, 3, 4, 5, 6, 7)
BF = jnp.bfloat16
F32 = jnp.float32


def leaky(values):
    return jnp.where(values > 0, values, 0.01 * values)


def kernel(
    volume, w1, b1, w2, b2, wi, bi, wo, bo,
    out,
    vbuf, w1b, w2b, wib, wob, b1b, b2b, bib, bob,
    lhs, sums, blocks, halo, inner, edge_out, edge_in, corner_out, corner_in,
    load_sem, send_sem, recv_sem,
):
    ix, iy = lax.axis_index("tx"), lax.axis_index("ty")
    nx, ny = lax.axis_size("tx"), lax.axis_size("ty")
    groups_x, groups_y = halo.shape[1] - 4, halo.shape[2] - 4
    half = groups_x * groups_y * 8

    def exists(d):
        dx, dy, _ = MESSAGES[d]
        test = None
        for delta, i, n in ((dx, ix, nx), (dy, iy, ny)):
            if delta:
                one = i >= 1 if delta < 0 else i <= n - 2
                test = one if test is None else jnp.logical_and(test, one)
        return test

    def device(d):
        return {"tx": ix + MESSAGES[d][0], "ty": iy + MESSAGES[d][1]}

    barrier = pltpu.get_barrier_semaphore()
    count = 0
    for d in NEIGHBOURS:
        count = count + exists(d).astype(jnp.int32)

        @pl.when(exists(d))
        def _():
            pl.semaphore_signal(
                barrier, inc=1, device_id=device(d), device_id_type=pl.DeviceIdType.MESH
            )

    loads = []

    def load(src, dst):
        copy = pltpu.make_async_copy(src, dst, load_sem.at[len(loads)])
        copy.start()
        loads.append(copy)
        return copy

    load_w1, load_b1 = load(w1, w1b), load(b1, b1b)
    units = vbuf.shape[0]
    load_v = [load(volume.at[pl.ds(4 * u, 4)], vbuf.at[u]) for u in range(units // 2)]
    load_w2, load_b2 = load(w2, w2b), load(b2, b2b)
    load_v += [load(volume.at[pl.ds(4 * u, 4)], vbuf.at[u]) for u in range(units // 2, units)]
    load_bi, load_bo = load(bi, bib), load(bo, bob)
    load_wi, load_wo = load(wi, wib), load(wo, wob)

    halo[...] = jnp.zeros_like(halo)

    load_w1.wait()
    load_b1.wait()
    w1cat = jnp.concatenate(
        [
            jnp.concatenate([w1b[p, q, 0], w1b[p, q, 1]], axis=1)
            for p in range(2)
            for q in range(2)
        ],
        axis=0,
    )
    rows_y = 2 * groups_y
    bias1 = b1b[...]

    def gather(u):
        slabs = [vbuf[u, j].reshape(rows_y, 4, 16, 64) for j in range(4)]
        for pc in range(2):
            for qc in range(2):
                lhs[u % 2, pc * 2 + qc] = jnp.concatenate(
                    [
                        slabs[2 * pc + p][:, 2 * qc + q].reshape(rows_y * 16, 64)
                        for p in range(2)
                        for q in range(2)
                    ],
                    axis=1,
                )

    def multiply(u):
        for k in range(4):
            both = jnp.dot(lhs[u % 2, k], w1cat, preferred_element_type=F32)
            sums[u * 4 + k, 0] = both[:, 0:128]
            sums[u * 4 + k, 1] = both[:, 128:256]

    def fold(u):
        row = u * 4 * rows_y
        for k in range(8):
            slot, rc = u * 4 + k // 2, k % 2
            even = sums[slot, 0, pl.ds(2 * rc, 4 * rows_y, stride=4)]
            odd = sums[slot, 1, pl.ds(2 * rc + 1, 4 * rows_y, stride=4)]
            finer = leaky(even + odd + bias1).astype(BF)
            blocks[row : row + 4 * rows_y, k * 128 : k * 128 + 128] = finer

    def copy_of(d, incoming):
        slot = d if incoming else PARTNER[d]
        if d < 2:
            src, dst = edge_out.at[d], edge_in.at[slot]
        else:
            src, dst = corner_out.at[d - 2], corner_in.at[slot - 2]
        return pltpu.make_async_remote_copy(
            src_ref=src,
            dst_ref=dst,
            send_sem=send_sem.at[d],
            recv_sem=recv_sem.at[slot],
            device_id=device(d),
            device_id_type=pl.DeviceIdType.MESH,
        )

    def landed(d):
        dx, dy, h = MESSAGES[d]
        if dx:
            px = slice(0, 2) if dx < 0 else slice(groups_x + 2, groups_x + 4)
        else:
            px = slice(2 + 2 * h, 4 + 2 * h)
        if dy:
            return px, slice(0, 2) if dy < 0 else slice(groups_y + 2, groups_y + 4)
        return px, slice(2, 2 + groups_y)

    def second(h):
        rows = half
        total = jnp.dot(
            blocks[h * rows : h * rows + rows],
            w2b[...].reshape(8 * 128, 256),
            preferred_element_type=F32,
        )
        coarse = leaky(total + b2b[...]).astype(BF).astype(F32)
        coarse = coarse.reshape(groups_x // 2, 2, groups_y * 8, 256)
        rows = half // 2
        even_x = coarse[:, 0].reshape(rows, 256)
        odd_x = coarse[:, 1].reshape(rows, 256)
        keep = (lax.broadcasted_iota(jnp.int32, (rows, 256), 0) // 2) % 2 == 0
        parts = [
            part.reshape(groups_x // 2, groups_y, 8, 256)
            for part in (
                jnp.where(keep, even_x, pltpu.roll(odd_x, 2, 0)),
                jnp.where(keep, pltpu.roll(even_x, rows - 2, 0), odd_x),
            )
        ]
        for d in SECOND if h else FIRST:
            dy = MESSAGES[d][1]
            sy = slice(0, 2) if dy < 0 else slice(groups_y - 2, groups_y) if dy else slice(0, groups_y)
            block = jnp.concatenate([p[:, sy].reshape(-1, 256) for p in parts], axis=0).astype(BF)
            if d < 2:
                edge_out[d] = block
            else:
                corner_out[d - 2] = block

            @pl.when(exists(d))
            def _():
                copy_of(d, False).start()

        for z in range(2):
            halo[z, 2 + 2 * h : 4 + 2 * h, 2 : 2 + groups_y] = parts[z]

    for t in range(units + 2):
        if t < units:
            load_v[t].wait()
            gather(t)
        if 1 <= t <= units:
            multiply(t - 1)
        if 2 <= t:
            fold(t - 2)
        if t == units // 2 + 1:
            load_w2.wait()
            load_b2.wait()
            pl.semaphore_wait(barrier, count)
            second(0)
        if t == units + 1:
            second(1)

    own = jnp.concatenate(
        [
            halo[z, 2 : 2 + groups_x, 2 : 2 + groups_y].reshape(half, 256).astype(BF)
            for z in range(2)
        ],
        axis=1,
    )
    keep = (lax.broadcasted_iota(jnp.int32, (half, 256), 0) // 2) % 2 == 0
    load_bi.wait()
    load_bo.wait()
    inner[...] = jnp.broadcast_to(bib[...].reshape(1, 1, 1, 1, 256), inner.shape)

    def both(lhs, weight, a, b):
        lower = weight[a, b, 1:3].reshape(512, 256)
        upper = weight[a, b, 0:2].reshape(512, 256)
        return (
            jnp.dot(lhs, lower, preferred_element_type=F32),
            jnp.dot(lhs, upper, preferred_element_type=F32),
        )

    def three(low_half, high_half, weight, a, b):
        shared = (low_half + high_half).astype(BF)
        return (
            jnp.dot(shared, weight[a, b, 1], preferred_element_type=F32),
            jnp.dot(high_half.astype(BF), weight[a, b, 2], preferred_element_type=F32),
            jnp.dot(low_half.astype(BF), weight[a, b, 0], preferred_element_type=F32),
        )

    def differences(weight):
        for a in range(3):
            for b in range(3):
                middle = weight[a, b, 1]
                weight[a, b, 0] = weight[a, b, 0] - middle
                weight[a, b, 2] = weight[a, b, 2] - middle

    load_wi.wait()
    for a in (1, 0, 2):
        for b in (1, 0, 2):
            for z, term in enumerate(both(own, wib, a, b)):
                inner[z, 2 - a : 2 - a + groups_x, 2 - b : 2 - b + groups_y] += term.reshape(
                    groups_x, groups_y, 8, 256
                )

    def receive(d, test=None):
        px, py = landed(d)
        there = exists(d)
        if test is not None:
            there = jnp.logical_and(there, test)

        @pl.when(there)
        def _():
            copy_of(d, True).wait_recv()
            block = (edge_in[d] if d < 2 else corner_in[d - 2]).astype(F32)
            rows = block.shape[0] // 2
            for z in range(2):
                shape = (px.stop - px.start, py.stop - py.start, 8, 256)
                halo[z, px, py] = block[z * rows : z * rows + rows].reshape(shape)

    core = lax.rem(ix, 2)

    def side(flip):
        def pick(even, odd):
            return even + flip * (odd - even)

        return (
            pick(groups_x + 2, 1),
            pick(groups_x + 3, 0),
            pick(groups_x + 1, 0),
            pick(groups_x, 1),
            pick(2, 0),
        )

    near_in, far_in, ring_in, edge_in_x, tap_in = side(core)
    near_out, far_out, ring_out, edge_out_x, tap_out = side(1 - core)

    def add(a, b, pieces):
        halves = [
            jnp.concatenate(
                [halo[z, pl.ds(g, n), sy].reshape(-1, 256) for g, n, sy, _ in pieces], axis=0
            )
            for z in range(2)
        ]
        shared, lower_only, upper_only = three(*halves, wib, a, b)
        for z, only in enumerate((lower_only, upper_only)):
            term = shared + only
            row = 0
            for _, n, sy, i in pieces:
                size = sy.stop - sy.start
                inner[z, pl.ds(i, n), sy.start - b : sy.stop - b] += term[
                    row : row + n * size * 8
                ].reshape(n, size, 8, 256)
                row += n * size * 8

    def present(i, edge):
        return jnp.where(i == edge, 0.0, 1.0).astype(F32)

    scale_x = {0: present(ix, 0), groups_x + 1: present(ix, nx - 1)}
    scale_y = {0: present(iy, 0), groups_y + 1: present(iy, ny - 1)}

    def activate(rows):
        for i in rows:
            for z in range(2):
                row = leaky(inner[z, i]).astype(BF).astype(F32)
                if i in scale_x:
                    row = row * scale_x[i]
                inner[z, i] = row
                for j, scale in scale_y.items():
                    inner[z, i, j] = row[j] * scale

    own_y = slice(2, 2 + groups_y)

    def surround(cols, near, far, ring, edge, tap, other):
        for b in range(3):
            inside = [j for j in cols if b <= j < b + groups_y + 2]
            for a in (1, tap, other):
                pieces = []
                if inside:
                    strip = slice(inside[0], inside[-1] + 1)
                    pieces.append((a, groups_x + 2, strip, 0))
                if a is tap:
                    pieces += [(near, 1, own_y, edge), (far, 1, own_y, ring)]
                elif a is not other:
                    pieces.append((near, 1, own_y, ring))
                if pieces:
                    add(a, b, pieces)

    load_wo.wait()
    differences(wib)
    differences(wob)
    for d in (2, 4, 6, 8):
        receive(d)
    receive(1, core == 0)
    receive(0, core == 1)
    surround((0, 1), near_in, far_in, ring_in, edge_in_x, tap_in, tap_out)
    for d in range(10):

        @pl.when(exists(d))
        def _():
            copy_of(d, False).wait_send()

    for d in (3, 5, 7, 9):
        receive(d)
    receive(0, core == 0)
    receive(1, core == 1)
    surround(
        (groups_y + 2, groups_y + 3),
        near_out, far_out, ring_out, edge_out_x, tap_out, tap_in,
    )
    activate(range(groups_x + 2))
    chains = [None] * 4
    for tap in range(9):
        a, b = tap // 3, tap % 3
        low_half, high_half = [
            inner[z, a : a + groups_x, b : b + groups_y].reshape(half, 256) for z in range(2)
        ]
        shared = low_half + high_half
        for k, lhs_in, c in (
            (0, high_half, 2),
            (1, low_half, 0),
            (2 + tap % 2, shared, 1),
        ):
            term = jnp.dot(lhs_in.astype(BF), wob[a, b, c], preferred_element_type=F32)
            chains[k] = term if chains[k] is None else chains[k] + term
    base = chains[2] + chains[3] * present(ix, -1) + bob[...]
    totals = [
        halo[z, 2 : 2 + groups_x, own_y].reshape(half, 256) + base + chains[z]
        for z in range(2)
    ]
    lower, upper = leaky(totals[0]), leaky(totals[1])
    even_x = jnp.where(keep, lower, pltpu.roll(upper, 2, 0)).astype(BF)
    odd_x = jnp.where(keep, pltpu.roll(lower, half - 2, 0), upper).astype(BF)
    rows = groups_y * 8
    for i in range(groups_x):
        for p, part in enumerate((even_x, odd_x)):
            out[2 * i + p] = part[i * rows : (i + 1) * rows].reshape(2 * groups_y, 4, 256)


def local(
    volume,
    first_weight,
    first_bias,
    second_weight,
    second_bias,
    inner_weight,
    inner_bias,
    outer_weight,
    outer_bias,
):
    size_x, size_y, size_z, chans = volume.shape
    gx, gy = size_x // 8, size_y // 8
    cells = gx * gy * 16
    any_spec = pl.BlockSpec(memory_space=pl.ANY)
    vmem = pltpu.VMEM
    result = pl.pallas_call(
        kernel,
        out_shape=pltpu.VMEM((size_x // 4, size_y // 4, size_z // 4, 256), BF),
        in_specs=[any_spec] * 9,
        out_specs=pl.BlockSpec(memory_space=pltpu.VMEM),
        scratch_shapes=[
            vmem((gx * 2, 4, size_y, size_z, chans), BF),
            vmem(first_weight.shape, BF),
            vmem(second_weight.shape, BF),
            vmem(inner_weight.shape, BF),
            vmem(outer_weight.shape, BF),
            vmem((1, 128), F32),
            vmem((1, 256), F32),
            vmem((1, 256), F32),
            vmem((1, 256), F32),
            vmem((2, 4, gy * 32, 256), BF),
            vmem((gx * 8, 2, gy * 32, 128), F32),
            vmem((cells, 1024), BF),
            vmem((2, gx + 4, gy + 4, 8, 256), F32),
            vmem((2, gx + 2, gy + 2, 8, 256), F32),
            vmem((2, gy * 32, 256), BF),
            vmem((2, gy * 32, 256), BF),
            vmem((8, 64, 256), BF),
            vmem((8, 64, 256), BF),
            pltpu.SemaphoreType.DMA((gx * 2 + 8,)),
            pltpu.SemaphoreType.DMA((10,)),
            pltpu.SemaphoreType.DMA((10,)),
        ],
        compiler_params=pltpu.CompilerParams(
            collective_id=0, has_side_effects=True, vmem_limit_bytes=56 * 2**20
        ),
        cost_estimate=pl.CostEstimate(
            flops=2_000_000_000, bytes_accessed=12_000_000, transcendentals=0
        ),
    )(
        volume,
        first_weight,
        first_bias.reshape(1, -1),
        second_weight,
        second_bias.reshape(1, -1),
        inner_weight,
        inner_bias.reshape(1, -1),
        outer_weight,
        outer_bias.reshape(1, -1),
    )
    return result


def solution(mesh):
    in_specs = (P("tx", "ty", None, None), P(), P(), P(), P(), P(), P(), P(), P())
    out_specs = P("tx", "ty", None, None)
    return jax.shard_map(local, mesh=mesh, in_specs=in_specs, out_specs=out_specs, check_vma=False)
```

```python
import jax
import jax.numpy as jnp
from jax import lax
from jax.experimental import pallas as pl
from jax.experimental.pallas import tpu as pltpu
from jax.sharding import PartitionSpec as P

MESSAGES = (
    (-1, 0, 0), (1, 0, 1),
    (-1, -1, 0), (-1, 1, 0), (0, -1, 0), (0, 1, 0),
    (1, -1, 1), (1, 1, 1), (0, -1, 1), (0, 1, 1),
)
PARTNER = (1, 0, 7, 6, 5, 4, 3, 2, 9, 8)
FIRST = (2, 3, 4, 5, 0)
SECOND = (8, 9, 6, 7, 1)
NEIGHBOURS = (0, 1, 2, 3, 4, 5, 6, 7)
BF = jnp.bfloat16
F32 = jnp.float32


def leaky(values):
    return jnp.maximum(values, 0.01 * values)


def kernel(
    volume, w1, b1, w2, b2, wi, bi, wo, bo,
    out,
    vbuf, w1b, w2b, wib, wob, b1b, b2b, bib, bob,
    lhs, sums, blocks, halo, inner, edge_out, edge_in, corner_out, corner_in,
    load_sem, send_sem, recv_sem,
):
    ix, iy = lax.axis_index("tx"), lax.axis_index("ty")
    nx, ny = lax.axis_size("tx"), lax.axis_size("ty")
    groups_x, groups_y = halo.shape[1] - 4, halo.shape[2] - 4
    half = groups_x * groups_y * 8

    def present(i, edge):
        return jnp.where(i == edge, 0.0, 1.0).astype(F32)

    one = present(ix, -1)

    def exists(d):
        dx, dy, _ = MESSAGES[d]
        test = None
        for delta, i, n in ((dx, ix, nx), (dy, iy, ny)):
            if delta:
                one = i >= 1 if delta < 0 else i <= n - 2
                test = one if test is None else jnp.logical_and(test, one)
        return test

    def device(d):
        return {"tx": ix + MESSAGES[d][0], "ty": iy + MESSAGES[d][1]}

    barrier = pltpu.get_barrier_semaphore()
    count = 0
    for d in NEIGHBOURS:
        count = count + exists(d).astype(jnp.int32)

        @pl.when(exists(d))
        def _():
            pl.semaphore_signal(
                barrier, inc=1, device_id=device(d), device_id_type=pl.DeviceIdType.MESH
            )

    loads = []

    def load(src, dst):
        copy = pltpu.make_async_copy(src, dst, load_sem.at[len(loads)])
        copy.start()
        loads.append(copy)
        return copy

    load_w1, load_b1 = load(w1, w1b), load(b1, b1b)
    units = vbuf.shape[0]
    load_v = [load(volume.at[u], vbuf.at[u]) for u in range(units // 2)]
    load_w2, load_b2 = load(w2, w2b), load(b2, b2b)
    load_v += [load(volume.at[u], vbuf.at[u]) for u in range(units // 2, units)]
    load_bi, load_bo = load(bi, bib), load(bo, bob)
    load_wi, load_wo = load(wi, wib), load(wo, wob)

    halo[...] = jnp.zeros_like(halo)

    load_w1.wait()
    load_b1.wait()
    w1cat = jnp.concatenate(
        [
            jnp.concatenate([w1b[p, q, 0], w1b[p, q, 1]], axis=1)
            for p in range(2)
            for q in range(2)
        ],
        axis=0,
    )
    rows_y = 2 * groups_y
    bias1 = b1b[...]

    def gather(u):
        slabs = [vbuf[u, j].reshape(rows_y, 4, 16, 64) for j in range(4)]
        for pc in range(2):
            for qc in range(2):
                lhs[u % 4, pc * 2 + qc] = jnp.concatenate(
                    [
                        slabs[2 * pc + p][:, 2 * qc + q].reshape(rows_y * 16, 64)
                        for p in range(2)
                        for q in range(2)
                    ],
                    axis=1,
                )

    def multiply(u):
        for k in range(4):
            both = jnp.dot(lhs[u % 4, k], w1cat, preferred_element_type=F32)
            sums[u * 4 + k, 0] = both[:, 0:128]
            sums[u * 4 + k, 1] = both[:, 128:256]

    def fold(u):
        row = u * 4 * rows_y
        for k in range(8):
            slot, rc = u * 4 + k // 2, k % 2
            even = sums[slot, 0, pl.ds(2 * rc, 4 * rows_y, stride=4)]
            odd = sums[slot, 1, pl.ds(2 * rc + 1, 4 * rows_y, stride=4)]
            finer = leaky(even + odd + bias1).astype(BF)
            blocks[row : row + 4 * rows_y, k * 128 : k * 128 + 128] = finer

    def copy_of(d, incoming):
        slot = d if incoming else PARTNER[d]
        if d < 2:
            src, dst = edge_out.at[d], edge_in.at[slot]
        else:
            src, dst = corner_out.at[d - 2], corner_in.at[slot - 2]
        return pltpu.make_async_remote_copy(
            src_ref=src,
            dst_ref=dst,
            send_sem=send_sem.at[d],
            recv_sem=recv_sem.at[slot],
            device_id=device(d),
            device_id_type=pl.DeviceIdType.MESH,
        )

    def landed(d):
        dx, dy, h = MESSAGES[d]
        if dx:
            px = slice(0, 2) if dx < 0 else slice(groups_x + 2, groups_x + 4)
        else:
            px = slice(2 + 2 * h, 4 + 2 * h)
        if dy:
            return px, slice(0, 2) if dy < 0 else slice(groups_y + 2, groups_y + 4)
        return px, slice(2, 2 + groups_y)

    keep = (lax.broadcasted_iota(jnp.int32, (1, 8, 256), 1) // 2) % 2 == 0

    def second(h):
        rows = half
        part = [
            jnp.dot(
                blocks[h * rows : h * rows + rows, k * 512 : k * 512 + 512],
                w2b[k].reshape(4 * 128, 256),
                preferred_element_type=F32,
            )
            for k in range(2)
        ]
        total = part[0] + part[1] * one
        coarse = leaky(total + b2b[...]).astype(BF).astype(F32)
        coarse = coarse.reshape(groups_x // 2, 2, groups_y * 8, 256)
        even_x = coarse[:, 0].reshape(-1, 8, 256)
        odd_x = coarse[:, 1].reshape(-1, 8, 256)
        parts = [
            part.reshape(groups_x // 2, groups_y, 8, 256)
            for part in (
                jnp.where(keep, even_x, pltpu.roll(odd_x, 2, 1)),
                jnp.where(keep, pltpu.roll(even_x, 6, 1), odd_x),
            )
        ]
        for z in range(2):
            halo[z, 2 + 2 * h : 4 + 2 * h, 2 : 2 + groups_y] = parts[z]
        messages = SECOND if h else FIRST
        for d in messages:
            dy = MESSAGES[d][1]
            sy = slice(0, 2) if dy < 0 else slice(groups_y - 2, groups_y) if dy else slice(0, groups_y)
            block = jnp.concatenate([p[:, sy].reshape(-1, 256) for p in parts], axis=0).astype(BF)
            if d < 2:
                edge_out[d] = block
            else:
                corner_out[d - 2] = block
        if not h:
            pl.semaphore_wait(barrier, count)
        for d in messages:

            @pl.when(exists(d))
            def _():
                copy_of(d, False).start()

    per_half = units // 2
    for h in range(2):
        rows = range(h * per_half, (h + 1) * per_half)
        early = rows[: per_half // 2] if h == 0 else rows
        for u in early:
            load_v[u].wait()
        for u in early:
            gather(u)
        for u in rows[len(early) :]:
            load_v[u].wait()
        if h == 0:
            load_w2.wait()
            load_b2.wait()
        for u in rows[len(early) :]:
            gather(u)
        for u in rows:
            multiply(u)
            fold(u)
        second(h)

    own = jnp.concatenate(
        [
            halo[z, 2 : 2 + groups_x, 2 : 2 + groups_y].reshape(half, 256).astype(BF)
            for z in range(2)
        ],
        axis=1,
    )
    load_bi.wait()
    load_bo.wait()
    inner[...] = jnp.broadcast_to(bib[...].reshape(1, 1, 1, 1, 256), inner.shape)

    def both(lhs, weight, a, b):
        lower = weight[a, b, 1:3].reshape(512, 256)
        upper = weight[a, b, 0:2].reshape(512, 256)
        return (
            jnp.dot(lhs, lower, preferred_element_type=F32),
            jnp.dot(lhs, upper, preferred_element_type=F32),
        )

    def differences(weight):
        for a in range(3):
            for b in range(3):
                middle = weight[a, b, 1]
                weight[a, b, 0] = weight[a, b, 0] - middle
                weight[a, b, 2] = weight[a, b, 2] - middle

    load_wi.wait()
    for a in (1, 0, 2):
        for b in (1, 0, 2):
            for z, term in enumerate(both(own, wib, a, b)):
                inner[z, 2 - a : 2 - a + groups_x, 2 - b : 2 - b + groups_y] += term.reshape(
                    groups_x, groups_y, 8, 256
                )

    def receive(d, test=None):
        px, py = landed(d)
        there = exists(d)
        if test is not None:
            there = jnp.logical_and(there, test)

        @pl.when(there)
        def _():
            copy_of(d, True).wait_recv()
            block = (edge_in[d] if d < 2 else corner_in[d - 2]).astype(F32)
            rows = block.shape[0] // 2
            for z in range(2):
                shape = (px.stop - px.start, py.stop - py.start, 8, 256)
                halo[z, px, py] = block[z * rows : z * rows + rows].reshape(shape)

    core = lax.rem(ix, 2)

    def side(flip):
        def pick(even, odd):
            return even + flip * (odd - even)

        return (
            pick(groups_x + 2, 1),
            pick(groups_x + 3, 0),
            pick(groups_x + 1, 0),
            pick(groups_x, 1),
            pick(2, 0),
        )

    side_in, side_out = side(core), side(1 - core)
    tap_in, tap_out = side_in[-1], side_out[-1]

    def add(a, b, pieces):
        lhs_halo = jnp.concatenate(
            [
                jnp.concatenate(
                    [halo[z, pl.ds(g, n), sy].reshape(-1, 256) for g, n, sy, _ in pieces],
                    axis=0,
                ).astype(BF)
                for z in range(2)
            ],
            axis=1,
        )
        for z, term in enumerate(both(lhs_halo, wib, a, b)):
            row = 0
            for _, n, sy, i in pieces:
                size = sy.stop - sy.start
                inner[z, pl.ds(i, n), sy.start - b : sy.stop - b] += term[
                    row : row + n * size * 8
                ].reshape(n, size, 8, 256)
                row += n * size * 8

    low_there, high_there = present(iy, 0), present(iy, ny - 1)
    out_there = jnp.where(core == 0, present(ix, 0), present(ix, nx - 1))

    def activate(x, cols, factor=None):
        for z in range(2):
            block = leaky(inner[z, x, cols]).astype(BF).astype(F32)
            if factor is not None:
                block = block * factor
            for j in range(cols.start, cols.stop):
                edge = {0: low_there, groups_y + 1: high_there}.get(j)
                value = block[j - cols.start]
                inner[z, x, j] = value if edge is None else value * edge

    own_y = slice(2, 2 + groups_y)

    def taps(b, inside, edge_of, roles):
        near, far, ring, edge, tap = edge_of
        for a in roles:
            pieces = []
            if inside:
                strip = slice(inside[0], inside[-1] + 1)
                pieces.append((a, groups_x + 2, strip, 0))
            if a is tap:
                pieces += [(near, 1, own_y, edge), (far, 1, own_y, ring)]
            elif isinstance(a, int):
                pieces.append((near, 1, own_y, ring))
            add(a, b, pieces)

    load_wo.wait()
    differences(wob)
    for d in (2, 4, 6, 8):
        receive(d)
    receive(1, core == 0)
    receive(0, core == 1)
    taps(0, (0, 1), side_in, (1, tap_in, tap_out))
    taps(1, (1,), side_in, (1, tap_in, tap_out))
    taps(2, (), side_in, (1, tap_in))
    for d in range(10):

        @pl.when(exists(d))
        def _():
            copy_of(d, False).wait_send()

    settled = 2 * (1 - core)
    for i in range(groups_x):
        activate(settled + i, slice(0, groups_y))
    for z in range(2):
        halo[z, 2 : 2 + groups_x, own_y] = halo[z, 2 : 2 + groups_x, own_y] + bob[...].reshape(
            1, 1, 1, 256
        )
    receive(0, core == 0)
    receive(1, core == 1)

    @pl.when(jnp.where(core == 0, ix, nx - 1 - ix) > 0)
    def _():
        taps(0, (), side_out, (1, tap_out))

    for d in (3, 5, 7, 9):
        receive(d)
    taps(1, (groups_y + 2,), side_out, (1, tap_out, tap_in))
    taps(2, (groups_y + 2, groups_y + 3), side_out, (1, tap_out, tap_in))
    for i in range(groups_x):
        activate(settled + i, slice(groups_y, groups_y + 2))
    open_x = groups_x * core
    for i in range(2):
        activate(
            open_x + i,
            slice(0, groups_y + 2),
            jnp.where(core == i, out_there, 1.0).astype(F32),
        )
    chains = [None] * 4
    for tap in range(9):
        a, b = tap // 3, tap % 3
        low_half, high_half = [
            inner[z, a : a + groups_x, b : b + groups_y].reshape(half, 256) for z in range(2)
        ]
        shared = low_half + high_half
        for k, lhs_in, c in (
            (0, high_half, 2),
            (1, low_half, 0),
            (2 + tap % 2, shared, 1),
        ):
            term = jnp.dot(lhs_in.astype(BF), wob[a, b, c], preferred_element_type=F32)
            chains[k] = term if chains[k] is None else chains[k] + term
    base = chains[2] + chains[3] * one
    totals = [
        halo[z, 2 : 2 + groups_x, own_y].reshape(half, 256) + base + chains[z]
        for z in range(2)
    ]
    lower, upper = [leaky(t).reshape(-1, 8, 256) for t in totals]
    even_x = jnp.where(keep, lower, pltpu.roll(upper, 2, 1)).reshape(half, 256).astype(BF)
    odd_x = jnp.where(keep, pltpu.roll(lower, 6, 1), upper).reshape(half, 256).astype(BF)
    rows = groups_y * 8
    for i in range(groups_x):
        for p, part in enumerate((even_x, odd_x)):
            out[2 * i + p] = part[i * rows : (i + 1) * rows].reshape(2 * groups_y, 4, 256)


def local(
    volume,
    first_weight,
    first_bias,
    second_weight,
    second_bias,
    inner_weight,
    inner_bias,
    outer_weight,
    outer_bias,
):
    size_x, size_y, size_z, chans = volume.shape
    gx, gy = size_x // 8, size_y // 8
    cells = gx * gy * 16
    any_spec = pl.BlockSpec(memory_space=pl.ANY)
    vmem = pltpu.VMEM
    result = pl.pallas_call(
        kernel,
        out_shape=pltpu.VMEM((size_x // 4, size_y // 4, size_z // 4, 256), BF),
        in_specs=[any_spec] * 9,
        out_specs=pl.BlockSpec(memory_space=pltpu.VMEM),
        scratch_shapes=[
            vmem((gx * 2, 4, size_y, size_z, chans), BF),
            vmem(first_weight.shape, BF),
            vmem(second_weight.shape, BF),
            vmem(inner_weight.shape, BF),
            vmem(outer_weight.shape, BF),
            vmem((1, 128), F32),
            vmem((1, 256), F32),
            vmem((1, 256), F32),
            vmem((1, 256), F32),
            vmem((4, 4, gy * 32, 256), BF),
            vmem((gx * 8, 2, gy * 32, 128), F32),
            vmem((cells, 1024), BF),
            vmem((2, gx + 4, gy + 4, 8, 256), F32),
            vmem((2, gx + 2, gy + 2, 8, 256), F32),
            vmem((2, gy * 32, 256), BF),
            vmem((2, gy * 32, 256), BF),
            vmem((8, 64, 256), BF),
            vmem((8, 64, 256), BF),
            pltpu.SemaphoreType.DMA((gx * 2 + 8,)),
            pltpu.SemaphoreType.DMA((10,)),
            pltpu.SemaphoreType.DMA((10,)),
        ],
        compiler_params=pltpu.CompilerParams(
            collective_id=0, has_side_effects=True, vmem_limit_bytes=56 * 2**20
        ),
        cost_estimate=pl.CostEstimate(
            flops=2_000_000_000, bytes_accessed=12_000_000, transcendentals=0
        ),
    )(
        volume.reshape(gx * 2, 4, size_y, size_z, chans),
        first_weight,
        first_bias.reshape(1, -1),
        second_weight,
        second_bias.reshape(1, -1),
        inner_weight,
        inner_bias.reshape(1, -1),
        outer_weight,
        outer_bias.reshape(1, -1),
    )
    return result


def solution(mesh):
    in_specs = (P("tx", "ty", None, None), P(), P(), P(), P(), P(), P(), P(), P())
    out_specs = P("tx", "ty", None, None)
    return jax.shard_map(local, mesh=mesh, in_specs=in_specs, out_specs=out_specs, check_vma=False)
```

```python
import jax
import jax.numpy as jnp
from jax import lax
from jax.experimental import pallas as pl
from jax.experimental.pallas import tpu as pltpu
from jax.sharding import PartitionSpec as P

MESSAGES = (
    (-1, 0, 0), (1, 0, 1),
    (-1, -1, 0), (-1, 1, 0), (0, -1, 0), (0, 1, 0),
    (1, -1, 1), (1, 1, 1), (0, -1, 1), (0, 1, 1),
)
PARTNER = (1, 0, 7, 6, 5, 4, 3, 2, 9, 8)
FIRST = (2, 3, 4, 5, 0)
SECOND = (8, 9, 6, 7, 1)
NEIGHBOURS = (0, 1, 2, 3, 4, 5, 6, 7)
BF = jnp.bfloat16
F32 = jnp.float32


def leaky(values):
    return jnp.maximum(values, 0.01 * values)


def kernel(
    volume, w1, b1, w2, b2, wi, bi, wo, bo,
    out,
    vbuf, w1b, w2b, wib, wob, b1b, b2b, bib, bob,
    lhs, sums, blocks, halo, inner, edge_out, edge_in, corner_out, corner_in,
    load_sem, send_sem, recv_sem,
):
    ix, iy = lax.axis_index("tx"), lax.axis_index("ty")
    nx, ny = lax.axis_size("tx"), lax.axis_size("ty")
    groups_x, groups_y = halo.shape[1] - 4, halo.shape[2] - 4
    half = groups_x * groups_y * 8

    def present(i, edge):
        return jnp.where(i == edge, 0.0, 1.0).astype(F32)

    one = present(ix, -1)

    def exists(d):
        dx, dy, _ = MESSAGES[d]
        test = None
        for delta, i, n in ((dx, ix, nx), (dy, iy, ny)):
            if delta:
                one = i >= 1 if delta < 0 else i <= n - 2
                test = one if test is None else jnp.logical_and(test, one)
        return test

    def device(d):
        return {"tx": ix + MESSAGES[d][0], "ty": iy + MESSAGES[d][1]}

    barrier = pltpu.get_barrier_semaphore()
    count = 0
    for d in NEIGHBOURS:
        count = count + exists(d).astype(jnp.int32)

        @pl.when(exists(d))
        def _():
            pl.semaphore_signal(
                barrier, inc=1, device_id=device(d), device_id_type=pl.DeviceIdType.MESH
            )

    loads = []

    def load(src, dst):
        copy = pltpu.make_async_copy(src, dst, load_sem.at[len(loads)])
        copy.start()
        loads.append(copy)
        return copy

    load_w1, load_b1 = load(w1, w1b), load(b1, b1b)
    units = vbuf.shape[0]
    load_v = [load(volume.at[u], vbuf.at[u]) for u in range(units // 2)]
    load_w2, load_b2 = load(w2, w2b), load(b2, b2b)
    load_v += [load(volume.at[u], vbuf.at[u]) for u in range(units // 2, units)]
    load_bi, load_bo = load(bi, bib), load(bo, bob)
    load_wi, load_wo = load(wi, wib), load(wo, wob)

    halo[...] = jnp.zeros_like(halo)

    load_w1.wait()
    load_b1.wait()
    w1cat = jnp.concatenate(
        [
            jnp.concatenate([w1b[p, q, 0], w1b[p, q, 1]], axis=1)
            for p in range(2)
            for q in range(2)
        ],
        axis=0,
    )
    rows_y = 2 * groups_y
    bias1 = b1b[...]

    def gather(u):
        slabs = [vbuf[u, j].reshape(rows_y, 4, 16, 64) for j in range(4)]
        for pc in range(2):
            for qc in range(2):
                lhs[u % 4, pc * 2 + qc] = jnp.concatenate(
                    [
                        slabs[2 * pc + p][:, 2 * qc + q].reshape(rows_y * 16, 64)
                        for p in range(2)
                        for q in range(2)
                    ],
                    axis=1,
                )

    def multiply(u):
        for k in range(4):
            both = jnp.dot(lhs[u % 4, k], w1cat, preferred_element_type=F32)
            sums[u * 4 + k, 0] = both[:, 0:128]
            sums[u * 4 + k, 1] = both[:, 128:256]

    def fold(u):
        row = u * 4 * rows_y
        for k in range(8):
            slot, rc = u * 4 + k // 2, k % 2
            even = sums[slot, 0, pl.ds(2 * rc, 4 * rows_y, stride=4)]
            odd = sums[slot, 1, pl.ds(2 * rc + 1, 4 * rows_y, stride=4)]
            finer = leaky(even + odd + bias1).astype(BF)
            blocks[row : row + 4 * rows_y, k * 128 : k * 128 + 128] = finer

    def copy_of(d, incoming):
        slot = d if incoming else PARTNER[d]
        if d < 2:
            src, dst = edge_out.at[d], edge_in.at[slot]
        else:
            src, dst = corner_out.at[d - 2], corner_in.at[slot - 2]
        return pltpu.make_async_remote_copy(
            src_ref=src,
            dst_ref=dst,
            send_sem=send_sem.at[d],
            recv_sem=recv_sem.at[slot],
            device_id=device(d),
            device_id_type=pl.DeviceIdType.MESH,
        )

    def landed(d):
        dx, dy, h = MESSAGES[d]
        if dx:
            px = slice(0, 2) if dx < 0 else slice(groups_x + 2, groups_x + 4)
        else:
            px = slice(2 + 2 * h, 4 + 2 * h)
        if dy:
            return px, slice(0, 2) if dy < 0 else slice(groups_y + 2, groups_y + 4)
        return px, slice(2, 2 + groups_y)

    keep = (lax.broadcasted_iota(jnp.int32, (1, 8, 256), 1) // 2) % 2 == 0

    def second(h):
        rows = half
        part = [
            jnp.dot(
                blocks[h * rows : h * rows + rows, k * 512 : k * 512 + 512],
                w2b[k].reshape(4 * 128, 256),
                preferred_element_type=F32,
            )
            for k in range(2)
        ]
        total = part[0] + part[1] * one
        coarse = leaky(total + b2b[...]).astype(BF).astype(F32)
        coarse = coarse.reshape(groups_x // 2, 2, groups_y * 8, 256)
        even_x = coarse[:, 0].reshape(-1, 8, 256)
        odd_x = coarse[:, 1].reshape(-1, 8, 256)
        parts = [
            part.reshape(groups_x // 2, groups_y, 8, 256)
            for part in (
                jnp.where(keep, even_x, pltpu.roll(odd_x, 2, 1)),
                jnp.where(keep, pltpu.roll(even_x, 6, 1), odd_x),
            )
        ]
        for z in range(2):
            halo[z, 2 + 2 * h : 4 + 2 * h, 2 : 2 + groups_y] = parts[z]
        messages = SECOND if h else FIRST
        for d in messages:
            dy = MESSAGES[d][1]
            sy = slice(0, 2) if dy < 0 else slice(groups_y - 2, groups_y) if dy else slice(0, groups_y)
            block = jnp.concatenate([p[:, sy].reshape(-1, 256) for p in parts], axis=0).astype(BF)
            if d < 2:
                edge_out[d] = block
            else:
                corner_out[d - 2] = block
        if not h:
            pl.semaphore_wait(barrier, count)
        for d in messages:

            @pl.when(exists(d))
            def _():
                copy_of(d, False).start()

    half_units = units // 2
    quarters = [range(k * units // 4, (k + 1) * units // 4) for k in range(4)]

    def take(rows):
        for u in rows:
            load_v[u].wait()
        for u in rows:
            gather(u)

    take(quarters[0])
    for h in range(2):
        take(quarters[2 * h + 1])
        for u in range(h * half_units, (h + 1) * half_units):
            multiply(u)
            fold(u)
        if h == 0:
            load_w2.wait()
            load_b2.wait()
            take(quarters[2])
        second(h)

    own = jnp.concatenate(
        [
            halo[z, 2 : 2 + groups_x, 2 : 2 + groups_y].reshape(half, 256).astype(BF)
            for z in range(2)
        ],
        axis=1,
    )
    load_bi.wait()
    load_bo.wait()
    inner[...] = jnp.broadcast_to(bib[...].reshape(1, 1, 1, 1, 256), inner.shape)

    def both(lhs, weight, a, b):
        lower = weight[a, b, 1:3].reshape(512, 256)
        upper = weight[a, b, 0:2].reshape(512, 256)
        return (
            jnp.dot(lhs, lower, preferred_element_type=F32),
            jnp.dot(lhs, upper, preferred_element_type=F32),
        )

    def differences(weight):
        for a in range(3):
            for b in range(3):
                middle = weight[a, b, 1]
                weight[a, b, 0] = weight[a, b, 0] - middle
                weight[a, b, 2] = weight[a, b, 2] - middle

    load_wi.wait()
    for a in (1, 0, 2):
        for b in (1, 0, 2):
            for z, term in enumerate(both(own, wib, a, b)):
                inner[z, 2 - a : 2 - a + groups_x, 2 - b : 2 - b + groups_y] += term.reshape(
                    groups_x, groups_y, 8, 256
                )

    def receive(d, test=None):
        px, py = landed(d)
        there = exists(d)
        if test is not None:
            there = jnp.logical_and(there, test)

        @pl.when(there)
        def _():
            copy_of(d, True).wait_recv()
            block = (edge_in[d] if d < 2 else corner_in[d - 2]).astype(F32)
            rows = block.shape[0] // 2
            for z in range(2):
                shape = (px.stop - px.start, py.stop - py.start, 8, 256)
                halo[z, px, py] = block[z * rows : z * rows + rows].reshape(shape)

    core = lax.rem(ix, 2)

    def side(flip):
        def pick(even, odd):
            return even + flip * (odd - even)

        return (
            pick(groups_x + 2, 1),
            pick(groups_x + 3, 0),
            pick(groups_x + 1, 0),
            pick(groups_x, 1),
            pick(2, 0),
        )

    side_in, side_out = side(core), side(1 - core)
    tap_in, tap_out = side_in[-1], side_out[-1]

    def add(a, b, pieces):
        lhs_halo = jnp.concatenate(
            [
                jnp.concatenate(
                    [halo[z, pl.ds(g, n), sy].reshape(-1, 256) for g, n, sy, _ in pieces],
                    axis=0,
                ).astype(BF)
                for z in range(2)
            ],
            axis=1,
        )
        for z, term in enumerate(both(lhs_halo, wib, a, b)):
            row = 0
            for _, n, sy, i in pieces:
                size = sy.stop - sy.start
                inner[z, pl.ds(i, n), sy.start - b : sy.stop - b] += term[
                    row : row + n * size * 8
                ].reshape(n, size, 8, 256)
                row += n * size * 8

    low_there, high_there = present(iy, 0), present(iy, ny - 1)
    out_there = jnp.where(core == 0, present(ix, 0), present(ix, nx - 1))

    def activate(x, cols, factor=None):
        for z in range(2):
            block = leaky(inner[z, x, cols]).astype(BF).astype(F32)
            if factor is not None:
                block = block * factor
            for j in range(cols.start, cols.stop):
                edge = {0: low_there, groups_y + 1: high_there}.get(j)
                value = block[j - cols.start]
                inner[z, x, j] = value if edge is None else value * edge

    own_y = slice(2, 2 + groups_y)

    def taps(b, inside, edge_of, roles):
        near, far, ring, edge, tap = edge_of
        for a in roles:
            pieces = []
            if inside:
                strip = slice(inside[0], inside[-1] + 1)
                pieces.append((a, groups_x + 2, strip, 0))
            if a is tap:
                pieces += [(near, 1, own_y, edge), (far, 1, own_y, ring)]
            elif isinstance(a, int):
                pieces.append((near, 1, own_y, ring))
            add(a, b, pieces)

    load_wo.wait()
    differences(wob)
    receive(1, core == 0)
    receive(0, core == 1)
    taps(2, (), side_in, (1, tap_in))
    for d in (2, 4, 6, 8):
        receive(d)
    taps(0, (0, 1), side_in, (1, tap_in, tap_out))
    taps(1, (1,), side_in, (1, tap_in, tap_out))
    for d in range(10):

        @pl.when(exists(d))
        def _():
            copy_of(d, False).wait_send()

    settled = 2 * (1 - core)
    for i in range(groups_x):
        activate(settled + i, slice(0, groups_y))
    for z in range(2):
        halo[z, 2 : 2 + groups_x, own_y] = halo[z, 2 : 2 + groups_x, own_y] + bob[...].reshape(
            1, 1, 1, 256
        )
    receive(0, core == 0)
    receive(1, core == 1)

    @pl.when(jnp.where(core == 0, ix, nx - 1 - ix) > 0)
    def _():
        taps(0, (), side_out, (1, tap_out))

    for d in (3, 5, 7, 9):
        receive(d)
    taps(1, (groups_y + 2,), side_out, (1, tap_out, tap_in))
    taps(2, (groups_y + 2, groups_y + 3), side_out, (1, tap_out, tap_in))
    for i in range(groups_x):
        activate(settled + i, slice(groups_y, groups_y + 2))
    open_x = groups_x * core
    for i in range(2):
        activate(
            open_x + i,
            slice(0, groups_y + 2),
            jnp.where(core == i, out_there, 1.0).astype(F32),
        )
    chains = [None] * 4
    for tap in range(9):
        a, b = tap // 3, tap % 3
        low_half, high_half = [
            inner[z, a : a + groups_x, b : b + groups_y].reshape(half, 256) for z in range(2)
        ]
        shared = low_half + high_half
        for k, lhs_in, c in (
            (0, high_half, 2),
            (1, low_half, 0),
            (2 + tap % 2, shared, 1),
        ):
            term = jnp.dot(lhs_in.astype(BF), wob[a, b, c], preferred_element_type=F32)
            chains[k] = term if chains[k] is None else chains[k] + term
    base = chains[2] + chains[3] * one
    totals = [
        halo[z, 2 : 2 + groups_x, own_y].reshape(half, 256) + base + chains[z]
        for z in range(2)
    ]
    lower, upper = [leaky(t).reshape(-1, 8, 256) for t in totals]
    even_x = jnp.where(keep, lower, pltpu.roll(upper, 2, 1)).reshape(half, 256).astype(BF)
    odd_x = jnp.where(keep, pltpu.roll(lower, 6, 1), upper).reshape(half, 256).astype(BF)
    rows = groups_y * 8
    for i in range(groups_x):
        for p, part in enumerate((even_x, odd_x)):
            out[2 * i + p] = part[i * rows : (i + 1) * rows].reshape(2 * groups_y, 4, 256)


def local(
    volume,
    first_weight,
    first_bias,
    second_weight,
    second_bias,
    inner_weight,
    inner_bias,
    outer_weight,
    outer_bias,
):
    size_x, size_y, size_z, chans = volume.shape
    gx, gy = size_x // 8, size_y // 8
    cells = gx * gy * 16
    any_spec = pl.BlockSpec(memory_space=pl.ANY)
    vmem = pltpu.VMEM
    result = pl.pallas_call(
        kernel,
        out_shape=pltpu.VMEM((size_x // 4, size_y // 4, size_z // 4, 256), BF),
        in_specs=[any_spec] * 9,
        out_specs=pl.BlockSpec(memory_space=pltpu.VMEM),
        scratch_shapes=[
            vmem((gx * 2, 4, size_y, size_z, chans), BF),
            vmem(first_weight.shape, BF),
            vmem(second_weight.shape, BF),
            vmem(inner_weight.shape, BF),
            vmem(outer_weight.shape, BF),
            vmem((1, 128), F32),
            vmem((1, 256), F32),
            vmem((1, 256), F32),
            vmem((1, 256), F32),
            vmem((4, 4, gy * 32, 256), BF),
            vmem((gx * 8, 2, gy * 32, 128), F32),
            vmem((cells, 1024), BF),
            vmem((2, gx + 4, gy + 4, 8, 256), F32),
            vmem((2, gx + 2, gy + 2, 8, 256), F32),
            vmem((2, gy * 32, 256), BF),
            vmem((2, gy * 32, 256), BF),
            vmem((8, 64, 256), BF),
            vmem((8, 64, 256), BF),
            pltpu.SemaphoreType.DMA((gx * 2 + 8,)),
            pltpu.SemaphoreType.DMA((10,)),
            pltpu.SemaphoreType.DMA((10,)),
        ],
        compiler_params=pltpu.CompilerParams(
            collective_id=0, has_side_effects=True, vmem_limit_bytes=56 * 2**20
        ),
        cost_estimate=pl.CostEstimate(
            flops=2_000_000_000, bytes_accessed=12_000_000, transcendentals=0
        ),
    )(
        volume.reshape(gx * 2, 4, size_y, size_z, chans),
        first_weight,
        first_bias.reshape(1, -1),
        second_weight,
        second_bias.reshape(1, -1),
        inner_weight,
        inner_bias.reshape(1, -1),
        outer_weight,
        outer_bias.reshape(1, -1),
    )
    return result


def solution(mesh):
    in_specs = (P("tx", "ty", None, None), P(), P(), P(), P(), P(), P(), P(), P())
    out_specs = P("tx", "ty", None, None)
    return jax.shard_map(local, mesh=mesh, in_specs=in_specs, out_specs=out_specs, check_vma=False)
```

```python
import jax
import jax.numpy as jnp
from jax import lax
from jax.experimental import pallas as pl
from jax.experimental.pallas import tpu as pltpu
from jax.sharding import PartitionSpec as P

MESSAGES = (
    (-1, 0, 0), (1, 0, 1),
    (-1, -1, 0), (-1, 1, 0), (0, -1, 0), (0, 1, 0),
    (1, -1, 1), (1, 1, 1), (0, -1, 1), (0, 1, 1),
)
PARTNER = (1, 0, 7, 6, 5, 4, 3, 2, 9, 8)
FIRST = (2, 3, 4, 5, 0)
SECOND = (8, 9, 6, 7, 1)
NEIGHBOURS = (0, 1, 2, 3, 4, 5, 6, 7)
BF = jnp.bfloat16
F32 = jnp.float32


def leaky(values):
    return jnp.maximum(values, 0.01 * values)


def kernel(
    volume, w1, b1, w2, b2, wi, bi, wo, bo,
    out,
    vbuf, w1b, w2b, wib, wob, b1b, b2b, bib, bob,
    lhs, sums, blocks, halo, inner, edge_out, edge_in, corner_out, corner_in,
    load_sem, send_sem, recv_sem,
):
    ix, iy = lax.axis_index("tx"), lax.axis_index("ty")
    nx, ny = lax.axis_size("tx"), lax.axis_size("ty")
    core = lax.rem(ix, 2)
    groups_x, groups_y = halo.shape[1] - 4, halo.shape[2] - 4
    half = groups_x * groups_y * 8

    def present(i, edge):
        return jnp.where(i == edge, 0.0, 1.0).astype(F32)

    one = present(ix, -1)

    def exists(d):
        dx, dy, _ = MESSAGES[d]
        test = None
        for delta, i, n in ((dx, ix, nx), (dy, iy, ny)):
            if delta:
                one = i >= 1 if delta < 0 else i <= n - 2
                test = one if test is None else jnp.logical_and(test, one)
        return test

    def device(d):
        return {"tx": ix + MESSAGES[d][0], "ty": iy + MESSAGES[d][1]}

    barrier = pltpu.get_barrier_semaphore()
    count = 0
    for d in NEIGHBOURS:
        count = count + exists(d).astype(jnp.int32)

        @pl.when(exists(d))
        def _():
            pl.semaphore_signal(
                barrier, inc=1, device_id=device(d), device_id_type=pl.DeviceIdType.MESH
            )

    loads = []

    def load(src, dst):
        copy = pltpu.make_async_copy(src, dst, load_sem.at[len(loads)])
        copy.start()
        loads.append(copy)
        return copy

    load_w1, load_b1 = load(w1, w1b), load(b1, b1b)
    units = vbuf.shape[0]
    quarters = [pl.ds(k * units // 4, units // 4) for k in range(4)]
    load_v = [load(volume.at[q], vbuf.at[q]) for q in quarters[:2]]
    load_w2, load_b2 = load(w2, w2b), load(b2, b2b)
    load_v += [load(volume.at[q], vbuf.at[q]) for q in quarters[2:]]
    load_bi, load_bo = load(bi, bib), load(bo, bob)
    load_wi, load_wo = load(wi, wib), load(wo, wob)

    halo[...] = jnp.zeros_like(halo)

    load_w1.wait()
    load_b1.wait()
    w1cat = jnp.concatenate(
        [
            jnp.concatenate([w1b[p, q, 0], w1b[p, q, 1]], axis=1)
            for p in range(2)
            for q in range(2)
        ],
        axis=0,
    )
    rows_y = 2 * groups_y
    bias1 = b1b[...]

    def gather(u):
        slabs = [vbuf[u, j].reshape(rows_y, 4, 16, 64) for j in range(4)]
        for pc in range(2):
            for qc in range(2):
                lhs[u % 4, pc * 2 + qc] = jnp.concatenate(
                    [
                        slabs[2 * pc + p][:, 2 * qc + q].reshape(rows_y * 16, 64)
                        for p in range(2)
                        for q in range(2)
                    ],
                    axis=1,
                )

    def multiply(u):
        for k in range(4):
            both = jnp.dot(lhs[u % 4, k], w1cat, preferred_element_type=F32)
            sums[u * 4 + k, 0] = both[:, 0:128]
            sums[u * 4 + k, 1] = both[:, 128:256]

    def fold(u):
        row = u * 4 * rows_y
        for k in range(8):
            slot, rc = u * 4 + k // 2, k % 2
            even = sums[slot, 0, pl.ds(2 * rc, 4 * rows_y, stride=4)]
            odd = sums[slot, 1, pl.ds(2 * rc + 1, 4 * rows_y, stride=4)]
            finer = leaky(even + odd + bias1).astype(BF)
            blocks[row : row + 4 * rows_y, k * 128 : k * 128 + 128] = finer

    def copy_of(d, incoming):
        slot = d if incoming else PARTNER[d]
        if d < 2:
            src, dst = edge_out.at[d], edge_in.at[slot]
        else:
            src, dst = corner_out.at[d - 2], corner_in.at[slot - 2]
        return pltpu.make_async_remote_copy(
            src_ref=src,
            dst_ref=dst,
            send_sem=send_sem.at[d],
            recv_sem=recv_sem.at[slot],
            device_id=device(d),
            device_id_type=pl.DeviceIdType.MESH,
        )

    def landed(d):
        dx, dy, h = MESSAGES[d]
        if dx:
            px = slice(0, 2) if dx < 0 else slice(groups_x + 2, groups_x + 4)
        else:
            px = slice(2 + 2 * h, 4 + 2 * h)
        if dy:
            return px, slice(0, 2) if dy < 0 else slice(groups_y + 2, groups_y + 4)
        return px, slice(2, 2 + groups_y)

    keep = (lax.broadcasted_iota(jnp.int32, (1, 8, 256), 1) // 2) % 2 == 0

    def send(d, test=None):
        there = exists(d)
        if test is not None:
            there = jnp.logical_and(there, test)

        @pl.when(there)
        def _():
            copy_of(d, False).start()

    def second(h):
        rows = half
        part = [
            jnp.dot(
                blocks[h * rows : h * rows + rows, k * 512 : k * 512 + 512],
                w2b[k].reshape(4 * 128, 256),
                preferred_element_type=F32,
            )
            for k in range(2)
        ]
        total = part[0] + part[1] * one
        coarse = leaky(total + b2b[...]).astype(BF).astype(F32)
        coarse = coarse.reshape(groups_x // 2, 2, groups_y * 8, 256)
        even_x = coarse[:, 0].reshape(-1, 8, 256)
        odd_x = coarse[:, 1].reshape(-1, 8, 256)
        parts = [
            part.reshape(groups_x // 2, groups_y, 8, 256)
            for part in (
                jnp.where(keep, even_x, pltpu.roll(odd_x, 2, 1)),
                jnp.where(keep, pltpu.roll(even_x, 6, 1), odd_x),
            )
        ]
        for z in range(2):
            halo[z, 2 + 2 * h : 4 + 2 * h, 2 : 2 + groups_y] = parts[z]
        messages = SECOND if h else FIRST
        for d in messages:
            dy = MESSAGES[d][1]
            sy = slice(0, 2) if dy < 0 else slice(groups_y - 2, groups_y) if dy else slice(0, groups_y)
            block = jnp.concatenate([p[:, sy].reshape(-1, 256) for p in parts], axis=0).astype(BF)
            if d < 2:
                edge_out[d] = block
            else:
                corner_out[d - 2] = block
        if not h:
            pl.semaphore_wait(barrier, count)
        edge, rest = messages[-1], messages[:-1]
        send(edge, core == edge)
        for d in rest:
            send(d)
        send(edge, core == 1 - edge)

    half_units = units // 2

    def take(k):
        load_v[k].wait()
        for u in range(k * units // 4, (k + 1) * units // 4):
            gather(u)

    take(0)
    for h in range(2):
        take(2 * h + 1)
        for u in range(h * half_units, (h + 1) * half_units):
            multiply(u)
            fold(u)
        if h == 0:
            load_w2.wait()
            load_b2.wait()
            take(2)
        second(h)

    own = jnp.concatenate(
        [
            halo[z, 2 : 2 + groups_x, 2 : 2 + groups_y].reshape(half, 256).astype(BF)
            for z in range(2)
        ],
        axis=1,
    )
    load_bi.wait()
    load_bo.wait()
    inner[...] = jnp.broadcast_to(bib[...].reshape(1, 1, 1, 1, 256), inner.shape)

    def both(lhs, weight, a, b):
        lower = weight[a, b, 1:3].reshape(512, 256)
        upper = weight[a, b, 0:2].reshape(512, 256)
        return (
            jnp.dot(lhs, lower, preferred_element_type=F32),
            jnp.dot(lhs, upper, preferred_element_type=F32),
        )

    def differences(weight):
        for a in range(3):
            for b in range(3):
                middle = weight[a, b, 1]
                weight[a, b, 0] = weight[a, b, 0] - middle
                weight[a, b, 2] = weight[a, b, 2] - middle

    load_wi.wait()
    for a in (1, 0, 2):
        for b in (1, 0, 2):
            for z, term in enumerate(both(own, wib, a, b)):
                inner[z, 2 - a : 2 - a + groups_x, 2 - b : 2 - b + groups_y] += term.reshape(
                    groups_x, groups_y, 8, 256
                )

    def receive(d, test=None):
        px, py = landed(d)
        there = exists(d)
        if test is not None:
            there = jnp.logical_and(there, test)

        @pl.when(there)
        def _():
            copy_of(d, True).wait_recv()
            block = (edge_in[d] if d < 2 else corner_in[d - 2]).astype(F32)
            rows = block.shape[0] // 2
            for z in range(2):
                shape = (px.stop - px.start, py.stop - py.start, 8, 256)
                halo[z, px, py] = block[z * rows : z * rows + rows].reshape(shape)

    def side(flip):
        def pick(even, odd):
            return even + flip * (odd - even)

        return (
            pick(groups_x + 2, 1),
            pick(groups_x + 3, 0),
            pick(groups_x + 1, 0),
            pick(groups_x, 1),
            pick(2, 0),
        )

    side_in, side_out = side(core), side(1 - core)
    tap_in, tap_out = side_in[-1], side_out[-1]

    def add(a, b, pieces):
        lhs_halo = jnp.concatenate(
            [
                jnp.concatenate(
                    [halo[z, pl.ds(g, n), sy].reshape(-1, 256) for g, n, sy, _ in pieces],
                    axis=0,
                ).astype(BF)
                for z in range(2)
            ],
            axis=1,
        )
        for z, term in enumerate(both(lhs_halo, wib, a, b)):
            row = 0
            for _, n, sy, i in pieces:
                size = sy.stop - sy.start
                inner[z, pl.ds(i, n), sy.start - b : sy.stop - b] += term[
                    row : row + n * size * 8
                ].reshape(n, size, 8, 256)
                row += n * size * 8

    low_there, high_there = present(iy, 0), present(iy, ny - 1)
    out_there = jnp.where(core == 0, present(ix, 0), present(ix, nx - 1))

    def activate(x, cols, factor=None):
        for z in range(2):
            block = leaky(inner[z, x, cols]).astype(BF).astype(F32)
            if factor is not None:
                block = block * factor
            for j in range(cols.start, cols.stop):
                edge = {0: low_there, groups_y + 1: high_there}.get(j)
                value = block[j - cols.start]
                inner[z, x, j] = value if edge is None else value * edge

    own_y = slice(2, 2 + groups_y)

    def taps(b, inside, edge_of, roles):
        near, far, ring, edge, tap = edge_of
        for a in roles:
            pieces = []
            if inside:
                strip = slice(inside[0], inside[-1] + 1)
                pieces.append((a, groups_x + 2, strip, 0))
            if a is tap:
                pieces += [(near, 1, own_y, edge), (far, 1, own_y, ring)]
            elif isinstance(a, int):
                pieces.append((near, 1, own_y, ring))
            add(a, b, pieces)

    load_wo.wait()
    differences(wob)
    receive(1, core == 0)
    receive(0, core == 1)
    taps(2, (), side_in, (1, tap_in))
    for d in (2, 4, 6, 8):
        receive(d)
    taps(0, (0, 1), side_in, (1, tap_in, tap_out))
    taps(1, (1,), side_in, (1, tap_in, tap_out))
    for d in range(10):

        @pl.when(exists(d))
        def _():
            copy_of(d, False).wait_send()

    settled = 2 * (1 - core)
    for i in range(groups_x):
        activate(settled + i, slice(0, groups_y))
    for z in range(2):
        halo[z, 2 : 2 + groups_x, own_y] = halo[z, 2 : 2 + groups_x, own_y] + bob[...].reshape(
            1, 1, 1, 256
        )
    receive(0, core == 0)
    receive(1, core == 1)

    @pl.when(jnp.where(core == 0, ix, nx - 1 - ix) > 0)
    def _():
        taps(0, (), side_out, (1, tap_out))

    for d in (3, 5, 7, 9):
        receive(d)
    taps(1, (groups_y + 2,), side_out, (1, tap_out, tap_in))
    taps(2, (groups_y + 2, groups_y + 3), side_out, (1, tap_out, tap_in))
    for i in range(groups_x):
        activate(settled + i, slice(groups_y, groups_y + 2))
    open_x = groups_x * core
    for i in range(2):
        activate(
            open_x + i,
            slice(0, groups_y + 2),
            jnp.where(core == i, out_there, 1.0).astype(F32),
        )
    chains = [None] * 4
    for tap in range(9):
        a, b = tap // 3, tap % 3
        low_half, high_half = [
            inner[z, a : a + groups_x, b : b + groups_y].reshape(half, 256) for z in range(2)
        ]
        shared = low_half + high_half
        for k, lhs_in, c in (
            (0, high_half, 2),
            (1, low_half, 0),
            (2 + tap % 2, shared, 1),
        ):
            term = jnp.dot(lhs_in.astype(BF), wob[a, b, c], preferred_element_type=F32)
            chains[k] = term if chains[k] is None else chains[k] + term
    base = chains[2] + chains[3] * one
    totals = [
        halo[z, 2 : 2 + groups_x, own_y].reshape(half, 256) + base + chains[z]
        for z in range(2)
    ]
    lower, upper = [leaky(t).reshape(-1, 8, 256) for t in totals]
    even_x = jnp.where(keep, lower, pltpu.roll(upper, 2, 1)).reshape(half, 256).astype(BF)
    odd_x = jnp.where(keep, pltpu.roll(lower, 6, 1), upper).reshape(half, 256).astype(BF)
    rows = groups_y * 8
    for i in range(groups_x):
        for p, part in enumerate((even_x, odd_x)):
            out[2 * i + p] = part[i * rows : (i + 1) * rows].reshape(2 * groups_y, 4, 256)


def local(
    volume,
    first_weight,
    first_bias,
    second_weight,
    second_bias,
    inner_weight,
    inner_bias,
    outer_weight,
    outer_bias,
):
    size_x, size_y, size_z, chans = volume.shape
    gx, gy = size_x // 8, size_y // 8
    cells = gx * gy * 16
    any_spec = pl.BlockSpec(memory_space=pl.ANY)
    vmem = pltpu.VMEM
    result = pl.pallas_call(
        kernel,
        out_shape=pltpu.VMEM((size_x // 4, size_y // 4, size_z // 4, 256), BF),
        in_specs=[any_spec] * 9,
        out_specs=pl.BlockSpec(memory_space=pltpu.VMEM),
        scratch_shapes=[
            vmem((gx * 2, 4, size_y, size_z, chans), BF),
            vmem(first_weight.shape, BF),
            vmem(second_weight.shape, BF),
            vmem(inner_weight.shape, BF),
            vmem(outer_weight.shape, BF),
            vmem((1, 128), F32),
            vmem((1, 256), F32),
            vmem((1, 256), F32),
            vmem((1, 256), F32),
            vmem((4, 4, gy * 32, 256), BF),
            vmem((gx * 8, 2, gy * 32, 128), F32),
            vmem((cells, 1024), BF),
            vmem((2, gx + 4, gy + 4, 8, 256), F32),
            vmem((2, gx + 2, gy + 2, 8, 256), F32),
            vmem((2, gy * 32, 256), BF),
            vmem((2, gy * 32, 256), BF),
            vmem((8, 64, 256), BF),
            vmem((8, 64, 256), BF),
            pltpu.SemaphoreType.DMA((12,)),
            pltpu.SemaphoreType.DMA((10,)),
            pltpu.SemaphoreType.DMA((10,)),
        ],
        compiler_params=pltpu.CompilerParams(
            collective_id=0, has_side_effects=True, vmem_limit_bytes=56 * 2**20
        ),
        cost_estimate=pl.CostEstimate(
            flops=2_000_000_000, bytes_accessed=12_000_000, transcendentals=0
        ),
    )(
        volume.reshape(gx * 2, 4, size_y, size_z, chans),
        first_weight,
        first_bias.reshape(1, -1),
        second_weight,
        second_bias.reshape(1, -1),
        inner_weight,
        inner_bias.reshape(1, -1),
        outer_weight,
        outer_bias.reshape(1, -1),
    )
    return result


def solution(mesh):
    in_specs = (P("tx", "ty", None, None), P(), P(), P(), P(), P(), P(), P(), P())
    out_specs = P("tx", "ty", None, None)
    return jax.shard_map(local, mesh=mesh, in_specs=in_specs, out_specs=out_specs, check_vma=False)
```

```python
import jax
import jax.numpy as jnp
from jax import lax
from jax.experimental import pallas as pl
from jax.experimental.pallas import tpu as pltpu
from jax.sharding import PartitionSpec as P

MESSAGES = (
    (-1, 0, 0), (1, 0, 1),
    (-1, -1, 0), (-1, 1, 0), (0, -1, 0), (0, 1, 0),
    (1, -1, 1), (1, 1, 1), (0, -1, 1), (0, 1, 1),
)
PARTNER = (1, 0, 7, 6, 5, 4, 3, 2, 9, 8)
FIRST = (2, 3, 4, 5, 0)
SECOND = (8, 9, 6, 7, 1)
NEIGHBOURS = (0, 1, 2, 3, 4, 5, 6, 7)
BF = jnp.bfloat16
F32 = jnp.float32


def leaky(values):
    return jnp.maximum(values, 0.01 * values)


def kernel(
    volume, w1, b1, w2, b2, wi, bi, wo, bo,
    out,
    vbuf, w1b, w2b, wib, wob, b1b, b2b, bib, bob,
    lhs, sums, blocks, halo, inner, edge_out, edge_in, corner_out, corner_in,
    load_sem, send_sem, recv_sem,
):
    ix, iy = lax.axis_index("tx"), lax.axis_index("ty")
    nx, ny = lax.axis_size("tx"), lax.axis_size("ty")
    core = lax.rem(ix, 2)
    groups_x, groups_y = halo.shape[1] - 4, halo.shape[2] - 4
    half = groups_x * groups_y * 8

    def present(i, edge):
        return jnp.where(i == edge, 0.0, 1.0).astype(F32)

    one = present(ix, -1)

    def exists(d):
        dx, dy, _ = MESSAGES[d]
        test = None
        for delta, i, n in ((dx, ix, nx), (dy, iy, ny)):
            if delta:
                one = i >= 1 if delta < 0 else i <= n - 2
                test = one if test is None else jnp.logical_and(test, one)
        return test

    def device(d):
        return {"tx": ix + MESSAGES[d][0], "ty": iy + MESSAGES[d][1]}

    barrier = pltpu.get_barrier_semaphore()
    count = 0
    for d in NEIGHBOURS:
        count = count + exists(d).astype(jnp.int32)

        @pl.when(exists(d))
        def _():
            pl.semaphore_signal(
                barrier, inc=1, device_id=device(d), device_id_type=pl.DeviceIdType.MESH
            )

    loads = []

    def load(src, dst):
        copy = pltpu.make_async_copy(src, dst, load_sem.at[len(loads)])
        copy.start()
        loads.append(copy)
        return copy

    load_w1, load_b1 = load(w1, w1b), load(b1, b1b)
    units = vbuf.shape[0]
    quarters = [pl.ds(k * units // 4, units // 4) for k in range(4)]
    load_v = [load(volume.at[q], vbuf.at[q]) for q in quarters[:2]]
    load_w2, load_b2 = load(w2, w2b), load(b2, b2b)
    load_v += [load(volume.at[q], vbuf.at[q]) for q in quarters[2:]]
    load_bi, load_bo = load(bi, bib), load(bo, bob)
    load_wi, load_wo = load(wi, wib), load(wo, wob)

    halo[...] = jnp.zeros_like(halo)

    load_w1.wait()
    load_b1.wait()
    w1cat = jnp.concatenate(
        [
            jnp.concatenate([w1b[p, q, 0], w1b[p, q, 1]], axis=1)
            for p in range(2)
            for q in range(2)
        ],
        axis=0,
    )
    rows_y = 2 * groups_y
    bias1 = b1b[...]

    def gather(u):
        slabs = [vbuf[u, j].reshape(rows_y, 4, 16, 64) for j in range(4)]
        for pc in range(2):
            for qc in range(2):
                lhs[u % 4, pc * 2 + qc] = jnp.concatenate(
                    [
                        slabs[2 * pc + p][:, 2 * qc + q].reshape(rows_y * 16, 64)
                        for p in range(2)
                        for q in range(2)
                    ],
                    axis=1,
                )

    def multiply(u):
        for k in range(4):
            both = jnp.dot(lhs[u % 4, k], w1cat, preferred_element_type=F32)
            sums[u * 4 + k, 0] = both[:, 0:128]
            sums[u * 4 + k, 1] = both[:, 128:256]

    def fold(u):
        row = u * 4 * rows_y
        for k in range(8):
            slot, rc = u * 4 + k // 2, k % 2
            even = sums[slot, 0, pl.ds(2 * rc, 4 * rows_y, stride=4)]
            odd = sums[slot, 1, pl.ds(2 * rc + 1, 4 * rows_y, stride=4)]
            finer = leaky(even + odd + bias1).astype(BF)
            blocks[row : row + 4 * rows_y, k * 128 : k * 128 + 128] = finer

    def copy_of(d, incoming):
        slot = d if incoming else PARTNER[d]
        if d < 2:
            src, dst = edge_out.at[d], edge_in.at[slot]
        else:
            src, dst = corner_out.at[d - 2], corner_in.at[slot - 2]
        return pltpu.make_async_remote_copy(
            src_ref=src,
            dst_ref=dst,
            send_sem=send_sem.at[d],
            recv_sem=recv_sem.at[slot],
            device_id=device(d),
            device_id_type=pl.DeviceIdType.MESH,
        )

    def landed(d):
        dx, dy, h = MESSAGES[d]
        if dx:
            px = slice(0, 2) if dx < 0 else slice(groups_x + 2, groups_x + 4)
        else:
            px = slice(2 + 2 * h, 4 + 2 * h)
        if dy:
            return px, slice(0, 2) if dy < 0 else slice(groups_y + 2, groups_y + 4)
        return px, slice(2, 2 + groups_y)

    keep = (lax.broadcasted_iota(jnp.int32, (1, 8, 256), 1) // 2) % 2 == 0

    def send(d, test=None):
        there = exists(d)
        if test is not None:
            there = jnp.logical_and(there, test)

        @pl.when(there)
        def _():
            copy_of(d, False).start()

    def second(h):
        rows = half
        part = [
            jnp.dot(
                blocks[h * rows : h * rows + rows, k * 512 : k * 512 + 512],
                w2b[k].reshape(4 * 128, 256),
                preferred_element_type=F32,
            )
            for k in range(2)
        ]
        total = part[0] + part[1] * one
        coarse = leaky(total + b2b[...]).astype(BF).astype(F32)
        coarse = coarse.reshape(groups_x // 2, 2, groups_y * 8, 256)
        even_x = coarse[:, 0].reshape(-1, 8, 256)
        odd_x = coarse[:, 1].reshape(-1, 8, 256)
        parts = [
            part.reshape(groups_x // 2, groups_y, 8, 256)
            for part in (
                jnp.where(keep, even_x, pltpu.roll(odd_x, 2, 1)),
                jnp.where(keep, pltpu.roll(even_x, 6, 1), odd_x),
            )
        ]
        for z in range(2):
            halo[z, 2 + 2 * h : 4 + 2 * h, 2 : 2 + groups_y] = parts[z]
        messages = SECOND if h else FIRST
        for d in messages:
            dy = MESSAGES[d][1]
            sy = slice(0, 2) if dy < 0 else slice(groups_y - 2, groups_y) if dy else slice(0, groups_y)
            block = jnp.concatenate([p[:, sy].reshape(-1, 256) for p in parts], axis=0).astype(BF)
            if d < 2:
                edge_out[d] = block
            else:
                corner_out[d - 2] = block
        if not h:
            pl.semaphore_wait(barrier, count)
        edge, rest = messages[-1], messages[:-1]
        send(edge, core == edge)
        for d in rest:
            send(d)
        send(edge, core == 1 - edge)

    half_units = units // 2

    def take(k):
        load_v[k].wait()
        for u in range(k * units // 4, (k + 1) * units // 4):
            gather(u)

    take(0)
    for h in range(2):
        take(2 * h + 1)
        for u in range(h * half_units, (h + 1) * half_units):
            multiply(u)
            fold(u)
        if h == 0:
            load_w2.wait()
            load_b2.wait()
            take(2)
        second(h)

    own = jnp.concatenate(
        [
            halo[z, 2 : 2 + groups_x, 2 : 2 + groups_y].reshape(half, 256).astype(BF)
            for z in range(2)
        ],
        axis=1,
    )
    load_bi.wait()
    load_bo.wait()
    inner[...] = jnp.broadcast_to(bib[...].reshape(1, 1, 1, 1, 256), inner.shape)

    def both(lhs, weight, a, b):
        lower = weight[a, b, 1:3].reshape(512, 256)
        upper = weight[a, b, 0:2].reshape(512, 256)
        return (
            jnp.dot(lhs, lower, preferred_element_type=F32),
            jnp.dot(lhs, upper, preferred_element_type=F32),
        )

    def differences(weight):
        for a in range(3):
            for b in range(3):
                middle = weight[a, b, 1]
                weight[a, b, 0] = weight[a, b, 0] - middle
                weight[a, b, 2] = weight[a, b, 2] - middle

    load_wi.wait()
    for a in (1, 0, 2):
        for b in (1, 0, 2):
            for z, term in enumerate(both(own, wib, a, b)):
                inner[z, 2 - a : 2 - a + groups_x, 2 - b : 2 - b + groups_y] += term.reshape(
                    groups_x, groups_y, 8, 256
                )

    def receive(d, test=None):
        px, py = landed(d)
        there = exists(d)
        if test is not None:
            there = jnp.logical_and(there, test)

        @pl.when(there)
        def _():
            copy_of(d, True).wait_recv()
            block = (edge_in[d] if d < 2 else corner_in[d - 2]).astype(F32)
            rows = block.shape[0] // 2
            for z in range(2):
                shape = (px.stop - px.start, py.stop - py.start, 8, 256)
                halo[z, px, py] = block[z * rows : z * rows + rows].reshape(shape)

    def side(flip):
        def pick(even, odd):
            return even + flip * (odd - even)

        return (
            pick(groups_x + 2, 1),
            pick(groups_x + 3, 0),
            pick(groups_x + 1, 0),
            pick(groups_x, 1),
            pick(2, 0),
        )

    side_in, side_out = side(core), side(1 - core)
    tap_in, tap_out = side_in[-1], side_out[-1]

    def add(a, b, pieces):
        lhs_halo = jnp.concatenate(
            [
                jnp.concatenate(
                    [halo[z, pl.ds(g, n), sy].reshape(-1, 256) for g, n, sy, _ in pieces],
                    axis=0,
                ).astype(BF)
                for z in range(2)
            ],
            axis=1,
        )
        for z, term in enumerate(both(lhs_halo, wib, a, b)):
            row = 0
            for _, n, sy, i in pieces:
                size = sy.stop - sy.start
                inner[z, pl.ds(i, n), sy.start - b : sy.stop - b] += term[
                    row : row + n * size * 8
                ].reshape(n, size, 8, 256)
                row += n * size * 8

    low_there, high_there = present(iy, 0), present(iy, ny - 1)
    out_there = jnp.where(core == 0, present(ix, 0), present(ix, nx - 1))

    def activate(x, cols, factor=None):
        for z in range(2):
            block = leaky(inner[z, x, cols]).astype(BF).astype(F32)
            if factor is not None:
                block = block * factor
            for j in range(cols.start, cols.stop):
                edge = {0: low_there, groups_y + 1: high_there}.get(j)
                value = block[j - cols.start]
                inner[z, x, j] = value if edge is None else value * edge

    own_y = slice(2, 2 + groups_y)

    def taps(b, inside, edge_of, roles):
        near, far, ring, edge, tap = edge_of
        for a in roles:
            pieces = []
            if inside:
                strip = slice(inside[0], inside[-1] + 1)
                pieces.append((a, groups_x + 2, strip, 0))
            if a is tap:
                pieces += [(near, 1, own_y, edge), (far, 1, own_y, ring)]
            elif isinstance(a, int):
                pieces.append((near, 1, own_y, ring))
            add(a, b, pieces)

    load_wo.wait()
    differences(wob)
    receive(1, core == 0)
    receive(0, core == 1)
    taps(2, (), side_in, (1, tap_in))
    for d in (2, 4, 6, 8):
        receive(d)
    taps(0, (0, 1), side_in, (1, tap_in, tap_out))
    taps(1, (1,), side_in, (1, tap_in, tap_out))
    for d in range(10):

        @pl.when(exists(d))
        def _():
            copy_of(d, False).wait_send()

    settled = 2 * (1 - core)
    for i in range(groups_x):
        activate(settled + i, slice(0, groups_y))
    for z in range(2):
        halo[z, 2 : 2 + groups_x, own_y] = halo[z, 2 : 2 + groups_x, own_y] + bob[...].reshape(
            1, 1, 1, 256
        )
    for d in (5, 7):
        receive(d)
    receive(0, core == 0)
    receive(1, core == 1)

    @pl.when(jnp.where(core == 0, ix, nx - 1 - ix) > 0)
    def _():
        taps(0, (), side_out, (1, tap_out))

    for d in (3, 9):
        receive(d)
    taps(2, (groups_y + 2, groups_y + 3), side_out, (1, tap_out, tap_in))
    taps(1, (groups_y + 2,), side_out, (1, tap_out, tap_in))
    for i in range(groups_x):
        activate(settled + i, slice(groups_y, groups_y + 2))
    open_x = groups_x * core
    for i in range(2):
        activate(
            open_x + i,
            slice(0, groups_y + 2),
            jnp.where(core == i, out_there, 1.0).astype(F32),
        )
    chains = [None] * 4
    for tap in range(9):
        a, b = tap // 3, tap % 3
        low_half, high_half = [
            inner[z, a : a + groups_x, b : b + groups_y].reshape(half, 256) for z in range(2)
        ]
        shared = low_half + high_half
        for k, lhs_in, c in (
            (0, high_half, 2),
            (1, low_half, 0),
            (2 + tap % 2, shared, 1),
        ):
            term = jnp.dot(lhs_in.astype(BF), wob[a, b, c], preferred_element_type=F32)
            chains[k] = term if chains[k] is None else chains[k] + term
    base = chains[2] + chains[3] * one
    totals = [
        halo[z, 2 : 2 + groups_x, own_y].reshape(half, 256) + base + chains[z]
        for z in range(2)
    ]
    lower, upper = [leaky(t).reshape(-1, 8, 256) for t in totals]
    even_x = jnp.where(keep, lower, pltpu.roll(upper, 2, 1)).reshape(half, 256).astype(BF)
    odd_x = jnp.where(keep, pltpu.roll(lower, 6, 1), upper).reshape(half, 256).astype(BF)
    rows = groups_y * 8
    for i in range(groups_x):
        for p, part in enumerate((even_x, odd_x)):
            out[2 * i + p] = part[i * rows : (i + 1) * rows].reshape(2 * groups_y, 4, 256)


def local(
    volume,
    first_weight,
    first_bias,
    second_weight,
    second_bias,
    inner_weight,
    inner_bias,
    outer_weight,
    outer_bias,
):
    size_x, size_y, size_z, chans = volume.shape
    gx, gy = size_x // 8, size_y // 8
    cells = gx * gy * 16
    any_spec = pl.BlockSpec(memory_space=pl.ANY)
    vmem = pltpu.VMEM
    result = pl.pallas_call(
        kernel,
        out_shape=pltpu.VMEM((size_x // 4, size_y // 4, size_z // 4, 256), BF),
        in_specs=[any_spec] * 9,
        out_specs=pl.BlockSpec(memory_space=pltpu.VMEM),
        scratch_shapes=[
            vmem((gx * 2, 4, size_y, size_z, chans), BF),
            vmem(first_weight.shape, BF),
            vmem(second_weight.shape, BF),
            vmem(inner_weight.shape, BF),
            vmem(outer_weight.shape, BF),
            vmem((1, 128), F32),
            vmem((1, 256), F32),
            vmem((1, 256), F32),
            vmem((1, 256), F32),
            vmem((4, 4, gy * 32, 256), BF),
            vmem((gx * 8, 2, gy * 32, 128), F32),
            vmem((cells, 1024), BF),
            vmem((2, gx + 4, gy + 4, 8, 256), F32),
            vmem((2, gx + 2, gy + 2, 8, 256), F32),
            vmem((2, gy * 32, 256), BF),
            vmem((2, gy * 32, 256), BF),
            vmem((8, 64, 256), BF),
            vmem((8, 64, 256), BF),
            pltpu.SemaphoreType.DMA((12,)),
            pltpu.SemaphoreType.DMA((10,)),
            pltpu.SemaphoreType.DMA((10,)),
        ],
        compiler_params=pltpu.CompilerParams(
            collective_id=0, has_side_effects=True, vmem_limit_bytes=56 * 2**20
        ),
        cost_estimate=pl.CostEstimate(
            flops=2_000_000_000, bytes_accessed=12_000_000, transcendentals=0
        ),
    )(
        volume.reshape(gx * 2, 4, size_y, size_z, chans),
        first_weight,
        first_bias.reshape(1, -1),
        second_weight,
        second_bias.reshape(1, -1),
        inner_weight,
        inner_bias.reshape(1, -1),
        outer_weight,
        outer_bias.reshape(1, -1),
    )
    return result


def solution(mesh):
    in_specs = (P("tx", "ty", None, None), P(), P(), P(), P(), P(), P(), P(), P())
    out_specs = P("tx", "ty", None, None)
    return jax.shard_map(local, mesh=mesh, in_specs=in_specs, out_specs=out_specs, check_vma=False)
```
